256 devices in a mesh: src: 16 (over z, x_hi), rcv: 16 (over x_lo, y, core).
Axes of the slice: x: 4 (x_hi: 2, x_lo: 2; x = x_hi * 2 + x_lo), y: 4, z: 8, core: 2. Of those that a mesh axis runs over, the one named last changes fastest.
Arguments:
- traces: bfloat16 [2, 1024, 3072], P(None, ('src', 'rcv')), may hold values from -6 to 6
- window_valid: int32 [2, 1024], P(None, ('src', 'rcv')), may hold values 0 or 1
- pair_mask: int32 [1024, 1024], P('src', 'rcv'), may hold values from 0 to 1, as said below
Outputs:
- correlations: float32 [1024, 1024, 512], P('src', 'rcv')
The draws below stay inside these ranges and needn't reach their ends.
Inputs may be any that keep to these rules, and one draw needn't show every extreme that they name: pair_mask[i, j] is 1 exactly where |i - j| lies in a band of offsets drawn for source channel i.
All inputs are finite; a program needn't handle non-finite values. No bound on the sum of `window_valid` on one device may be relied on, other than what follows from the above.
Results may differ from the reference program's by a relative error of at most 0.0064.
Values may be sent and summed in bfloat16 or wider, within the bound.
A program may use at most 128 MiB of HBM per device.

```python
import math
import jax
import jax.numpy as jnp
from jax import lax

CH = 1024
NS = 3072
NF = 1536
LAGS = 512
HALF = 32
WIN = 2


def draw_pair_mask(key, part):
    key = jax.random.fold_in(key, 3)
    low_key, span_key = jax.random.split(key)
    lowest = jax.random.randint(low_key, (CH, 1), 0, 64)
    spread = jax.random.randint(span_key, (CH, 1), 32, 256)
    row_ids = lax.broadcasted_iota(jnp.int32, (CH, CH), 0)
    col_ids = lax.broadcasted_iota(jnp.int32, (CH, CH), 1)
    offset = jnp.abs(row_ids - col_ids)
    inside = (offset >= lowest) & (offset <= lowest + spread)
    return inside.astype(jnp.int32)


def set_ends(drawn, rng, smallest, high):
    spot = [jax.random.randint(jax.random.fold_in(rng, axis), (), 0, length) for axis, length in enumerate(drawn.shape)]
    longest = drawn.shape.index(max(drawn.shape))
    neighbour = spot[:longest] + [(spot[longest] + 1) % drawn.shape[longest]] + spot[longest + 1:]
    return drawn.at[tuple(spot)].set(smallest).at[tuple(neighbour)].set(high)


def level_of(key, shape, cuts, smallest, top_value):
    def one(dim, blocks):
        draws = jax.random.uniform(jax.random.fold_in(jax.random.fold_in(key, 6), dim), (blocks,), jnp.float32, smallest / len(cuts), top_value / len(cuts))
        return jnp.repeat(jnp.exp(draws), shape[dim] // blocks).reshape((-1,) + (1,) * (len(shape) - dim - 1))

    loudness = one(*cuts[0])
    for cut in cuts[1:]:
        loudness = loudness * one(*cut)
    return loudness


def scatter_about(own_key, shape, scale, limit, pieces=(), held_as=jnp.bfloat16):
    drawn = jax.random.normal(own_key, shape, jnp.float32) * scale
    if len(pieces) > 0:
        drawn = level_of(own_key, shape, pieces, -0.22, 0.18) * drawn
    return jnp.clip(drawn, min=-limit, max=limit).astype(held_as)


def setup_inputs(seed: int = 0) -> dict:
    arg_keys = jax.random.split(jax.random.key(seed), 4)
    return {
        "traces": scatter_about(arg_keys[0], (WIN, CH, NS), 1.0, 6.0, ((1, 256),)),
        "window_valid": set_ends((jax.random.randint(arg_keys[1], (WIN, CH), 0, 8) < 7).astype(jnp.int32), jax.random.fold_in(arg_keys[1], 1), 0, 1),
        "pair_mask": draw_pair_mask(jax.random.fold_in(arg_keys[3], 71), 0),
    }


EPSILON = 1e-06

def fourier_table(samples, freq_count):
    sample_ids = lax.broadcasted_iota(jnp.int32, (samples, freq_count), 0)
    freq_ids = lax.broadcasted_iota(jnp.int32, (samples, freq_count), 1) + 1
    phases = sample_ids * freq_ids % samples
    angles = phases.astype(jnp.float32) * (2.0 * math.pi / samples)
    return jnp.concatenate([jnp.cos(angles), -jnp.sin(angles)], axis=1).astype(jnp.bfloat16)

def lag_table(samples, freq_count, lag_count):
    freq_ids = lax.broadcasted_iota(jnp.int32, (freq_count, lag_count), 0) + 1
    lag_ids = lax.broadcasted_iota(jnp.int32, (freq_count, lag_count), 1) - lag_count // 2
    phases = jnp.mod(freq_ids * lag_ids, samples)
    angles = phases.astype(jnp.float32) * (2.0 * math.pi / samples)
    return jnp.concatenate([jnp.cos(angles), -jnp.sin(angles)], axis=0).astype(jnp.bfloat16)

def whiten(traces, flags, table, half_width):
    win_count, chan_count, sample_count = traces.shape
    freq_count = table.shape[1] // 2
    spectrum = jnp.dot(traces.reshape(win_count * chan_count, sample_count), table, preferred_element_type=jnp.float32)
    real_part = spectrum[:, :freq_count]
    imag_part = spectrum[:, freq_count:]
    amplitude = jnp.sqrt(real_part * real_part + imag_part * imag_part)
    running = lax.reduce_window(amplitude, jnp.zeros((), amplitude.dtype), lax.add, (1, 2 * half_width + 1), (1, 1), ((0, 0), (half_width, half_width)))
    running = running / (2 * half_width + 1)
    factor = flags.reshape(win_count * chan_count, 1).astype(jnp.float32) / (running + EPSILON)
    whitened = spectrum * jnp.concatenate([factor, factor], axis=1)
    return whitened.astype(jnp.bfloat16).reshape(win_count, chan_count, 2 * freq_count)

def correlate(sources, receivers, source_flags, receiver_flags, mask_block, lags):
    freq_count = sources.shape[2] // 2
    counts = jnp.dot(source_flags.T, receiver_flags, preferred_element_type=jnp.float32)
    src_real = sources[:, :, None, :freq_count].astype(jnp.float32)
    src_imag = sources[:, :, None, freq_count:].astype(jnp.float32)
    rcv_real = receivers[:, None, :, :freq_count].astype(jnp.float32)
    rcv_imag = receivers[:, None, :, freq_count:].astype(jnp.float32)
    cross_real = lax.optimization_barrier(jnp.sum(src_real * rcv_real + src_imag * rcv_imag, axis=0))
    cross_imag = lax.optimization_barrier(jnp.sum(src_imag * rcv_real - src_real * rcv_imag, axis=0))
    scale = 1.0 / jnp.maximum(counts, 1.0)
    stacked = (jnp.concatenate([cross_real, cross_imag], axis=2) * scale[:, :, None]).astype(jnp.bfloat16)
    src_count, rcv_count = counts.shape
    result = jnp.dot(stacked.reshape(src_count * rcv_count, 2 * freq_count), lags, preferred_element_type=jnp.float32)
    weight = mask_block.astype(jnp.float32)[:, :, None] * (1.0 / math.sqrt(freq_count))
    return result.reshape(src_count, rcv_count, lags.shape[1]) * weight

def reference(traces, window_valid, pair_mask):
    whitened = whiten(traces, window_valid, fourier_table(NS, NF), HALF)
    flags = window_valid.astype(jnp.float32)
    lags = lag_table(NS, NF, LAGS)
    block_rows = 16

    def one_block(block_index):
        start = (block_index * block_rows).astype(jnp.int32)
        sources = lax.dynamic_slice_in_dim(whitened, start, block_rows, 1)
        source_flags = lax.dynamic_slice_in_dim(flags, start, block_rows, 1)
        mask_rows = lax.dynamic_slice_in_dim(pair_mask, start, block_rows, 0)
        return correlate(sources, whitened, source_flags, flags, mask_rows, lags)
    result = lax.map(one_block, jnp.arange(CH // block_rows, dtype=jnp.int32))
    return result.reshape(CH, CH, LAGS)
```

```python
import functools
import math

import jax
import jax.numpy as jnp
import numpy as np
from jax import lax
from jax.experimental import pallas as pl
from jax.experimental.pallas import tpu as pltpu
from jax.sharding import PartitionSpec as P

NS = 3072
NF = 1536
LAGS = 512
HALF = 32
WIN = 2
EPSILON = 1e-06
STEP = 2.0 * math.pi / NS
INVALID = 100.0
F32 = jnp.float32
BF16 = jnp.bfloat16
VMEM = pl.BlockSpec(memory_space=pltpu.VMEM)


def cos_sin(angles):
    return np.stack([np.cos(angles), np.sin(angles)]).astype(np.float32)


def seeds():
    freqs = np.arange(1, NF + 1, dtype=np.float64) * STEP
    halves = np.arange(LAGS // 2, dtype=np.float64) + 0.5
    first = cos_sin(np.arange(16)[:, None] * freqs[None, :])
    turn = cos_sin(np.broadcast_to(16 * freqs, (8, NF)))
    phase = cos_sin(np.broadcast_to(0.5 * freqs, (8, NF)))
    lag_first = cos_sin(freqs[:16, None] * halves[None, :])
    lag_turn = cos_sin(np.broadcast_to(16 * STEP * halves, (8, LAGS // 2)))
    return first, turn, phase, lag_first, lag_turn


def rotate(cosine, sine, turn_cos, turn_sin):
    return cosine * turn_cos - sine * turn_sin, sine * turn_cos + cosine * turn_sin


def fill_forward(first_ref, turn_ref, table):
    width = 512
    for block in range(NF // width):
        lanes = pl.ds(block * width, width)
        imag_lanes = pl.ds(NF + block * width, width)
        turn_cos, turn_sin = turn_ref[0, 0:1, lanes], turn_ref[1, 0:1, lanes]

        def rows(index, held):
            cosine, sine = held
            at = pl.ds(pl.multiple_of(index * 16, 16), 16)
            table[at, lanes] = cosine.astype(BF16)
            table[at, imag_lanes] = (-sine).astype(BF16)
            return rotate(cosine, sine, turn_cos, turn_sin)

        lax.fori_loop(0, NS // 32, rows, (first_ref[0, :, lanes], first_ref[1, :, lanes]))


def fill_lags(first_ref, turn_ref, cos_table, sin_table):
    turn_cos, turn_sin = turn_ref[0, 0:1, :], turn_ref[1, 0:1, :]

    def rows(index, held):
        cosine, sine = held
        at = pl.ds(pl.multiple_of(index * 16, 16), 16)
        cos_table[at, :] = cosine.astype(BF16)
        sin_table[at, :] = sine.astype(BF16)
        return rotate(cosine, sine, turn_cos, turn_sin)

    lax.fori_loop(0, NF // 16, rows, (first_ref[0], first_ref[1]))


def whiten_kernel(
    count, pieces_ref, first_ref, turn_ref, phase_ref, lag_first_ref, lag_turn_ref,
    src_ref, rcv_ref, flags_ref, cos_ref, sin_ref, table, ordered, left, spectrum, high, low
):
    half = count // 2
    fill_forward(first_ref, turn_ref, table)
    fill_lags(lag_first_ref, lag_turn_ref, cos_ref, sin_ref)
    for piece in range(count // 4):
        rows = pieces_ref[piece].astype(F32)
        for part in range(4):
            ordered[part, 4 * piece : 4 * piece + 4, :] = rows[4 * part : 4 * part + 4]
    lane = lax.broadcasted_iota(jnp.int32, (count, 128), 1)
    flags = jnp.zeros((count, 128), F32)
    for window in range(WIN):
        valid = ordered[window, :, 0:1] < 0.5 * INVALID
        flags = jnp.where((lane == window) & valid, 1.0, flags)
        for part in (window, WIN + window):
            left[pl.ds(part * count, count), :] = jnp.where(valid, ordered[part], 0.0).astype(BF16)
    flags_ref[...] = flags
    total = WIN * count
    width = 256
    even = lax.broadcasted_iota(jnp.int32, (1, width), 1) % 2 == 0
    for ref in (high, low):
        ref[:, 0:128] = jnp.zeros((total, 128), BF16)
        ref[:, 128 + NF : 256 + NF] = jnp.zeros((total, 128), BF16)

    def transform(block, carry):
        at = pl.multiple_of(block * width, width)
        square = None
        for base in (0, NF):
            lanes = pl.ds(pl.multiple_of(base + at, width), width)
            both = jnp.dot(left[...], table[:, lanes], preferred_element_type=F32)
            later = both[total:]
            value = both[:total] + jnp.where(even, -later, later)
            spectrum[:, lanes] = value
            square = value * value if square is None else square + value * value
        amplitude = jnp.sqrt(square)
        rounded = amplitude.astype(BF16)
        lanes = pl.ds(pl.multiple_of(128 + at, 128), width)
        high[:, lanes] = rounded
        low[:, lanes] = (amplitude - rounded.astype(F32)).astype(BF16)
        return carry

    lax.fori_loop(0, NF // width, transform, 0)
    offset = lax.broadcasted_iota(jnp.int32, (2 * width, width), 0) - lax.broadcasted_iota(
        jnp.int32, (2 * width, width), 1
    )
    band = jnp.where((offset >= 128 - HALF) & (offset <= 128 + HALF), 1.0, 0.0).astype(BF16)

    def smooth(block, carry):
        at = pl.multiple_of(block * width, width)
        around = pl.ds(at, 2 * width)
        running = jnp.dot(high[:, around], band, preferred_element_type=F32)
        running += jnp.dot(low[:, around], band, preferred_element_type=F32)
        factor = 1.0 / (running * (1.0 / (2 * HALF + 1)) + EPSILON)
        real_lanes = pl.ds(at, width)
        imag_lanes = pl.ds(pl.multiple_of(NF + at, width), width)
        real = (spectrum[:, real_lanes] * factor).astype(BF16)
        imag = (spectrum[:, imag_lanes] * factor).astype(BF16)
        turn_cos, turn_sin = phase_ref[0, 0:1, real_lanes], phase_ref[1, 0:1, real_lanes]
        for window in range(WIN):
            start = window * count
            src_real = real[start : start + half].astype(F32)
            src_imag = imag[start : start + half].astype(F32)
            src_ref[window, :, real_lanes] = src_real * turn_cos + src_imag * turn_sin
            src_ref[window, :, imag_lanes] = src_imag * turn_cos - src_real * turn_sin
            rcv_ref[window, :, real_lanes] = real[start + half : start + count]
            rcv_ref[window, :, imag_lanes] = imag[start + half : start + count]
        return carry

    lax.fori_loop(0, NF // width, smooth, 0)


def whitened(pieces):
    first, turn, phase, lag_first, lag_turn = seeds()
    count = pieces.shape[0] * 4
    half = count // 2
    return pl.pallas_call(
        functools.partial(whiten_kernel, count),
        out_shape=[
            jax.ShapeDtypeStruct((WIN, half, NS), F32),
            jax.ShapeDtypeStruct((WIN, half, NS), BF16),
            jax.ShapeDtypeStruct((count, 128), F32),
            jax.ShapeDtypeStruct((NF, LAGS // 2), BF16),
            jax.ShapeDtypeStruct((NF, LAGS // 2), BF16),
        ],
        in_specs=[VMEM] * 6,
        out_specs=[VMEM] * 5,
        scratch_shapes=[
            pltpu.VMEM((NS // 2, NS), BF16),
            pltpu.VMEM((4, count, NS // 2), F32),
            pltpu.VMEM((4 * count, NS // 2), BF16),
            pltpu.VMEM((WIN * count, NS), F32),
            pltpu.VMEM((WIN * count, NF + 256), BF16),
            pltpu.VMEM((WIN * count, NF + 256), BF16),
        ],
        compiler_params=pltpu.CompilerParams(vmem_limit_bytes=56 * 2**20),
    )(pieces, first, turn, phase, lag_first, lag_turn)


CHUNK = 4


def correlate_kernel(steps, src_ref, rcv_ref, flags_ref, mask_ref, cos_ref, sin_ref, out_ref,
                     weights, real_a, imag_a, real_b, imag_b):
    step = pl.program_id(0)
    half = rcv_ref.shape[1]
    rows = CHUNK * half
    groups = half // 16

    @pl.when(step == 0)
    def _():
        counts = lax.dot_general(
            flags_ref[half:, :].astype(BF16), flags_ref[:half, :].astype(BF16),
            (((1,), (1,)), ((), ())), preferred_element_type=F32)
        by_receiver = mask_ref[...].astype(F32).T
        weights[:, :half] = by_receiver * (1.0 / math.sqrt(NF)) / jnp.maximum(counts, 1.0)

    def cross(real_buf, imag_buf, inside):
        eight = lax.div(jnp.minimum(step, steps - 1) * CHUNK, 8)
        for block in range(NF // 128):
            real_lanes = slice(block * 128, block * 128 + 128)
            imag_lanes = slice(NF + block * 128, NF + block * 128 + 128)
            received = [
                [
                    (rcv_ref[w, 16 * g : 16 * g + 16, real_lanes], rcv_ref[w, 16 * g : 16 * g + 16, imag_lanes])
                    for w in range(WIN)
                ]
                for g in range(groups)
            ]
            for source in range(CHUNK):
                at = slice(inside + source, inside + source + 1)
                sent = [
                    tuple(
                        jnp.broadcast_to(src_ref[w, eight, at, lanes], (16, 128)).astype(BF16)
                        for lanes in (real_lanes, imag_lanes)
                    )
                    for w in range(WIN)
                ]
                for g in range(groups):
                    real = imag = None
                    for w in range(WIN):
                        (ar, ai), (br, bi) = sent[w], received[g][w]
                        more_real = ar * br + ai * bi
                        more_imag = ai * br - ar * bi
                        real = more_real if real is None else real + more_real
                        imag = more_imag if imag is None else imag + more_imag
                    place = slice(source * half + 16 * g, source * half + 16 * g + 16)
                    real_buf[place, real_lanes] = real
                    imag_buf[place, real_lanes] = imag

    def lags(real_buf, imag_buf):
        width = LAGS // 2
        even = jnp.dot(real_buf[...], cos_ref[...], preferred_element_type=F32)
        odd = jnp.dot(imag_buf[...], sin_ref[...], preferred_element_type=F32)
        first = jnp.maximum(step - 1, 0) * CHUNK
        near = pltpu.roll(weights[...], lax.rem(128 - first, 128), 1)
        back = 127 - lax.broadcasted_iota(jnp.int32, (half, 128), 1)
        for source in range(CHUNK):
            place = slice(source * half, source * half + half)
            weight = jnp.broadcast_to(near[:, source : source + 1], (half, 128))
            for block in range(width // 128):
                lanes = slice(block * 128, block * 128 + 128)
                e, o = even[place, lanes], odd[place, lanes]
                out_ref[source, :, width + block * 128 : width + block * 128 + 128] = (e - o) * weight
                flipped = jnp.take_along_axis((e + o) * weight, back, axis=1)
                out_ref[source, :, width - block * 128 - 128 : width - block * 128] = flipped

    @pl.when(step % 2 == 0)
    def _():
        lags(real_b, imag_b)
        cross(real_a, imag_a, 0)

    @pl.when(step % 2 == 1)
    def _():
        lags(real_a, imag_a)
        cross(real_b, imag_b, CHUNK % 8)


def correlated(src, rcv, flags, mask, cos_table, sin_table):
    half = rcv.shape[1]
    steps = half // CHUNK
    whole = lambda a: pl.BlockSpec(a.shape, lambda s: (0,) * a.ndim, pipeline_mode=pl.Buffered(1))
    args = (src.reshape(WIN, half // 8, 8, NS), rcv, flags, mask, cos_table, sin_table)
    buffers = [pltpu.VMEM((CHUNK * half, NF), BF16)] * 4
    return pl.pallas_call(
        functools.partial(correlate_kernel, steps),
        grid=(steps + 1,),
        out_shape=jax.ShapeDtypeStruct((half, half, LAGS), F32),
        in_specs=[whole(a) for a in args],
        out_specs=pl.BlockSpec((CHUNK, half, LAGS), lambda s: (jnp.maximum(s - 1, 0), 0, 0)),
        scratch_shapes=[pltpu.VMEM((half, 128), F32)] + buffers,
        compiler_params=pltpu.CompilerParams(vmem_limit_bytes=48 * 2**20),
    )(*args)

MESH = pl.DeviceIdType.MESH


def gather_kernel(side, mine_ref, out_ref, send_sems, recv_sems):
    s, r = lax.axis_index("src"), lax.axis_index("rcv")
    barrier = pltpu.get_barrier_semaphore()

    def greet_row(k, carry):
        pl.semaphore_signal(barrier, inc=1, device_id=(s, lax.rem(r + k, side)), device_id_type=MESH)
        return carry

    def greet_senders(k, carry):
        pl.semaphore_signal(barrier, inc=1, device_id=(r, lax.rem(s + k, side)), device_id_type=MESH)
        return carry

    lax.fori_loop(1, side, greet_row, 0)
    lax.fori_loop(1, side, greet_senders, 0)

    @pl.when(s != r)
    def _():
        pl.semaphore_signal(barrier, inc=1, device_id=(r, s), device_id_type=MESH)

    pl.semaphore_wait(barrier, 2 * (side - 1) + jnp.where(s == r, 0, 1))

    def column(k):
        return pltpu.make_async_remote_copy(
            src_ref=mine_ref, dst_ref=out_ref.at[side + r],
            send_sem=send_sems.at[1], recv_sem=recv_sems.at[1],
            device_id=(lax.rem(s + k, side), s), device_id_type=MESH)

    def row(k):
        return pltpu.make_async_remote_copy(
            src_ref=mine_ref, dst_ref=out_ref.at[r],
            send_sem=send_sems.at[0], recv_sem=recv_sems.at[0],
            device_id=(s, lax.rem(r + k, side)), device_id_type=MESH)

    def send(k, carry):
        column(k).start()
        row(k).start()
        return carry

    own = pltpu.make_async_copy(mine_ref, out_ref.at[r], recv_sems.at[0])
    own.start()
    lax.fori_loop(1, side, send, 0)
    first = pltpu.make_async_remote_copy(
        src_ref=mine_ref, dst_ref=out_ref.at[side + r],
        send_sem=send_sems.at[2], recv_sem=recv_sems.at[1],
        device_id=(s, s), device_id_type=MESH)

    @pl.when(s != r)
    def _():
        first.start()

    @pl.when(s == r)
    def _():
        pltpu.make_async_copy(mine_ref, out_ref.at[side + r], recv_sems.at[1]).start()

    for half in range(2):
        block = out_ref.at[pl.ds(half * side, side)]
        pltpu.make_async_copy(block, block, recv_sems.at[half]).wait()
        block = out_ref.at[pl.ds(0, side - 1)]
        pltpu.make_async_copy(block, block, send_sems.at[half]).wait()

    @pl.when(s != r)
    def _():
        first.wait_send()


def gathered(side, mine):
    return pl.pallas_call(
        functools.partial(gather_kernel, side),
        out_shape=jax.ShapeDtypeStruct((2 * side,) + mine.shape, mine.dtype),
        in_specs=[VMEM],
        out_specs=VMEM,
        scratch_shapes=[pltpu.SemaphoreType.DMA((3,)), pltpu.SemaphoreType.DMA((2,))],
        compiler_params=pltpu.CompilerParams(collective_id=0, has_side_effects=True),
    )(mine)


def shards(side, traces, window_valid, pair_mask):
    marked = jnp.where(window_valid[:, :, None] != 0, traces, jnp.asarray(INVALID, traces.dtype))
    windows, channels, samples = traces.shape
    mine = marked.reshape(windows, channels, 2, samples // 2).transpose(2, 0, 1, 3)
    mine = mine.reshape(2 * windows * channels, samples // 2)
    pieces = gathered(side, mine)
    src, rcv, flags, cos_table, sin_table = whitened(pieces)
    return correlated(src, rcv, flags, pair_mask, cos_table, sin_table)


def solution(mesh):
    in_specs = (P(None, ("src", "rcv"), None), P(None, ("src", "rcv")), P("src", "rcv"))
    return jax.shard_map(
        functools.partial(shards, mesh.shape["src"]),
        mesh=mesh, in_specs=in_specs, out_specs=P("src", "rcv", None), check_vma=False)
```

```python
import functools
import math

import jax
import jax.numpy as jnp
import numpy as np
from jax import lax
from jax.experimental import pallas as pl
from jax.experimental.pallas import tpu as pltpu
from jax.sharding import PartitionSpec as P

NS = 3072
NF = 1536
LAGS = 512
HALF = 32
WIN = 2
EPSILON = 1e-06
STEP = 2.0 * math.pi / NS
INVALID = 100.0
F32 = jnp.float32
BF16 = jnp.bfloat16
VMEM = pl.BlockSpec(memory_space=pltpu.VMEM)


def cos_sin(angles):
    return np.stack([np.cos(angles), np.sin(angles)]).astype(np.float32)


def seeds():
    freqs = np.arange(1, NF + 1, dtype=np.float64) * STEP
    halves = np.arange(LAGS // 2, dtype=np.float64) + 0.5
    first = cos_sin(np.arange(16)[:, None] * freqs[None, :])
    turn = cos_sin(np.broadcast_to(16 * freqs, (8, NF)))
    phase = cos_sin(np.broadcast_to(0.5 * freqs, (8, NF)))
    lag_first = cos_sin(freqs[:16, None] * halves[None, :])
    lag_turn = cos_sin(np.broadcast_to(16 * STEP * halves, (8, LAGS // 2)))
    return first, turn, phase, lag_first, lag_turn


def rotate(cosine, sine, turn_cos, turn_sin):
    return cosine * turn_cos - sine * turn_sin, sine * turn_cos + cosine * turn_sin


def fill_forward(first_ref, turn_ref, table, block, width):
    lanes = pl.ds(block * width, width)
    imag_lanes = pl.ds(NF + block * width, width)
    turn_cos, turn_sin = turn_ref[0, 0:1, lanes], turn_ref[1, 0:1, lanes]

    def rows(index, held):
        cosine, sine = held
        at = pl.ds(pl.multiple_of(index * 16, 16), 16)
        table[at, lanes] = cosine.astype(BF16)
        table[at, imag_lanes] = (-sine).astype(BF16)
        return rotate(cosine, sine, turn_cos, turn_sin)

    lax.fori_loop(0, NS // 32, rows, (first_ref[0, :, lanes], first_ref[1, :, lanes]))


def fill_lags(first_ref, turn_ref, cos_table, sin_table):
    turn_cos, turn_sin = turn_ref[0, 0:1, :], turn_ref[1, 0:1, :]

    def rows(index, held):
        cosine, sine = held
        at = pl.ds(pl.multiple_of(index * 16, 16), 16)
        cos_table[at, :] = cosine.astype(BF16)
        sin_table[at, :] = sine.astype(BF16)
        return rotate(cosine, sine, turn_cos, turn_sin)

    lax.fori_loop(0, NF // 16, rows, (first_ref[0], first_ref[1]))


def channel_group(slot):
    if slot < 16:
        core, low, y = slot // 8, slot // 4 % 2, slot % 4
        return 8 * low + 2 * y + core
    return 16 + slot % 8 * 2 + (slot - 16) // 8


def whiten_kernel(
    count, pieces_ref, table, phase_ref, src_ref, rcv_ref, flags_ref, ordered, left, spectrum, high, low
):
    half = count // 2
    for piece in range(count // 4):
        rows = pieces_ref[piece].astype(F32)
        first = 4 * channel_group(piece)
        for part in range(4):
            ordered[part, first : first + 4, :] = rows[4 * part : 4 * part + 4]
    lane = lax.broadcasted_iota(jnp.int32, (count, 128), 1)
    flags = jnp.zeros((count, 128), F32)
    for window in range(WIN):
        valid = ordered[window, :, 0:1] < 0.5 * INVALID
        flags = jnp.where((lane == window) & valid, 1.0, flags)
        for part in (window, WIN + window):
            left[pl.ds(part * count, count), :] = jnp.where(valid, ordered[part], 0.0).astype(BF16)
    flags_ref[...] = flags
    total = WIN * count
    width = 256
    even = lax.broadcasted_iota(jnp.int32, (1, width), 1) % 2 == 0
    for ref in (high, low):
        ref[:, 0:128] = jnp.zeros((total, 128), BF16)
        ref[:, 128 + NF : 256 + NF] = jnp.zeros((total, 128), BF16)

    def transform(block, carry):
        at = pl.multiple_of(block * width, width)
        square = None
        for base in (0, NF):
            lanes = pl.ds(pl.multiple_of(base + at, width), width)
            both = jnp.dot(left[...], table[:, lanes], preferred_element_type=F32)
            later = both[total:]
            value = both[:total] + jnp.where(even, -later, later)
            spectrum[:, lanes] = value
            square = value * value if square is None else square + value * value
        amplitude = jnp.sqrt(square)
        rounded = amplitude.astype(BF16)
        lanes = pl.ds(pl.multiple_of(128 + at, 128), width)
        high[:, lanes] = rounded
        low[:, lanes] = (amplitude - rounded.astype(F32)).astype(BF16)
        return carry

    lax.fori_loop(0, NF // width, transform, 0)
    offset = lax.broadcasted_iota(jnp.int32, (2 * width, width), 0) - lax.broadcasted_iota(
        jnp.int32, (2 * width, width), 1
    )
    band = jnp.where((offset >= 128 - HALF) & (offset <= 128 + HALF), 1.0, 0.0).astype(BF16)

    def smooth(block, carry):
        at = pl.multiple_of(block * width, width)
        around = pl.ds(at, 2 * width)
        running = jnp.dot(high[:, around], band, preferred_element_type=F32)
        running += jnp.dot(low[:, around], band, preferred_element_type=F32)
        factor = 1.0 / (running * (1.0 / (2 * HALF + 1)) + EPSILON)
        real_lanes = pl.ds(at, width)
        imag_lanes = pl.ds(pl.multiple_of(NF + at, width), width)
        real = (spectrum[:, real_lanes] * factor).astype(BF16)
        imag = (spectrum[:, imag_lanes] * factor).astype(BF16)
        turn_cos, turn_sin = phase_ref[0, 0:1, real_lanes], phase_ref[1, 0:1, real_lanes]
        for window in range(WIN):
            start = window * count
            src_real = real[start : start + half].astype(F32)
            src_imag = imag[start : start + half].astype(F32)
            src_ref[window, :, real_lanes] = src_real * turn_cos + src_imag * turn_sin
            src_ref[window, :, imag_lanes] = src_imag * turn_cos - src_real * turn_sin
            rcv_ref[window, :, real_lanes] = real[start + half : start + count]
            rcv_ref[window, :, imag_lanes] = imag[start + half : start + count]
        return carry

    lax.fori_loop(0, NF // width, smooth, 0)


def whitened(pieces, table, phase):
    count = pieces.shape[0] * 4
    half = count // 2
    return pl.pallas_call(
        functools.partial(whiten_kernel, count),
        out_shape=[
            jax.ShapeDtypeStruct((WIN, half, NS), F32),
            jax.ShapeDtypeStruct((WIN, half, NS), BF16),
            jax.ShapeDtypeStruct((count, 128), F32),
        ],
        in_specs=[VMEM] * 3,
        out_specs=[VMEM] * 3,
        scratch_shapes=[
            pltpu.VMEM((4, count, NS // 2), F32),
            pltpu.VMEM((4 * count, NS // 2), BF16),
            pltpu.VMEM((WIN * count, NS), F32),
            pltpu.VMEM((WIN * count, NF + 256), BF16),
            pltpu.VMEM((WIN * count, NF + 256), BF16),
        ],
        compiler_params=pltpu.CompilerParams(vmem_limit_bytes=18 * 2**20),
    )(pieces, table, phase)


CHUNK = 8
WIDE = 256


def correlate_kernel(src_ref, rcv_ref, flags_ref, mask_ref, cos_ref, sin_ref, out_ref,
                     weights, staged, out_sems):
    half = rcv_ref.shape[1]
    steps = half // CHUNK
    groups = half // 16
    blocks = NF // WIDE

    across = flags_ref[:half, :].T
    counts = sum(flags_ref[half:, w : w + 1] * across[w : w + 1, :] for w in range(WIN))
    by_receiver = mask_ref[...].astype(F32).T
    weights[:, :half] = by_receiver * (1.0 / math.sqrt(NF)) / jnp.maximum(counts, 1.0)
    weights[:, half:] = jnp.zeros((half, 128 - half), F32)
    back = 127 - lax.broadcasted_iota(jnp.int32, (half, 128), 1)

    def finish(even_acc, odd_acc, near, source, slot):
        even, odd = pltpu.matmul_pop(even_acc), pltpu.matmul_pop(odd_acc)
        weight = jnp.broadcast_to(near[:, source : source + 1], (half, 128))
        width = LAGS // 2
        for block in range(width // 128):
            lanes = slice(block * 128, block * 128 + 128)
            e, o = even[:, lanes], odd[:, lanes]
            staged[slot, source, :, width + block * 128 : width + block * 128 + 128] = (e - o) * weight
            flipped = jnp.take_along_axis((e + o) * weight, back, axis=1)
            staged[slot, source, :, width - block * 128 - 128 : width - block * 128] = flipped

    def cross(eight, inside, block):
        real_rows, imag_rows = [], []
        halves = []
        for part in range(WIDE // 128):
            first = block * WIDE + part * 128
            lanes = (slice(first, first + 128), slice(NF + first, NF + first + 128))
            sent = [
                [
                    jnp.broadcast_to(src_ref[w, eight, inside : inside + 1, at], (16, 128)).astype(BF16)
                    for at in lanes
                ]
                for w in range(WIN)
            ]
            halves.append((lanes, sent))
        for g in range(groups):
            reals, imags = [], []
            for lanes, sent in halves:
                real = imag = None
                for w in range(WIN):
                    ar, ai = sent[w]
                    br, bi = (rcv_ref[w, 16 * g : 16 * g + 16, at] for at in lanes)
                    more_real = ar * br + ai * bi
                    more_imag = ai * br - ar * bi
                    real = more_real if real is None else real + more_real
                    imag = more_imag if imag is None else imag + more_imag
                reals.append(real)
                imags.append(imag)
            real_rows.append(jnp.concatenate(reals, axis=1))
            imag_rows.append(jnp.concatenate(imags, axis=1))
        return jnp.concatenate(real_rows, axis=0), jnp.concatenate(imag_rows, axis=0)

    def near_of(chunk):
        return pltpu.roll(weights[...], lax.rem(256 - chunk * CHUNK, 128), 1)

    def put(chunk):
        slot = chunk % 2 if isinstance(chunk, int) else lax.rem(chunk, 2)
        at = pl.ds(pl.multiple_of(chunk * CHUNK, CHUNK), CHUNK)
        return pltpu.make_async_copy(staged.at[slot], out_ref.at[at], out_sems.at[slot])

    def with_accumulators(even_accs, odd_accs):
        def do_chunk(chunk, now, finishing):
            near = near_of(chunk - 1)
            slot = 1 - now

            @pl.when(chunk >= 3)
            def _():
                put(chunk - 3).wait()

            done = 0
            for block in range(blocks):
                rows = pl.ds(block * WIDE, WIDE)
                pltpu.matmul_push_rhs(cos_ref[rows, :], block % 2, 0)
                pltpu.matmul_push_rhs(sin_ref[rows, :], block % 2, 1)
                for source in range(CHUNK):
                    if finishing and (block * CHUNK + source) * CHUNK >= done * blocks * CHUNK and done < CHUNK:
                        finish(even_accs[slot][done], odd_accs[slot][done], near, done, slot)
                        done += 1
                    real, imag = cross(chunk * (CHUNK // 8) + source // 8, source % 8, block)
                    load = block % 2 if source == 0 else None
                    pltpu.matmul_acc_lhs(even_accs[now][source], real, load_staged_rhs=load)
                    pltpu.matmul_acc_lhs(odd_accs[now][source], imag, load_staged_rhs=load)

            @pl.when(chunk >= 1)
            def _():
                put(chunk - 1).start()

        def step(pair, carry):
            do_chunk(2 * pair, 0, True)
            do_chunk(2 * pair + 1, 1, True)
            return carry

        zero = jnp.zeros((half, WIDE), BF16)
        for unit, (table, accs) in enumerate(((cos_ref, even_accs), (sin_ref, odd_accs))):
            pltpu.matmul_push_rhs(table[0:WIDE, :], 0, unit)
            for source in range(CHUNK):
                pltpu.matmul_acc_lhs(accs[1][source], zero, load_staged_rhs=0 if source == 0 else None)
        lax.fori_loop(0, steps // 2, step, 0)
        last = steps - 1
        put(last - 2).wait()
        near = near_of(last)
        for source in range(CHUNK):
            finish(even_accs[1][source], odd_accs[1][source], near, source, last % 2)
        put(last).start()
        put(last - 1).wait()
        put(last).wait()

    pl.run_scoped(
        with_accumulators,
        [[pltpu.ACC(0)((half, LAGS // 2), F32) for _ in range(CHUNK)] for _ in range(2)],
        [[pltpu.ACC(1)((half, LAGS // 2), F32) for _ in range(CHUNK)] for _ in range(2)],
    )


def correlated(src, rcv, flags, mask, cos_table, sin_table):
    half = rcv.shape[1]
    args = (src.reshape(WIN, half // 8, 8, NS), rcv, flags, mask, cos_table, sin_table)
    return pl.pallas_call(
        correlate_kernel,
        out_shape=jax.ShapeDtypeStruct((half, half, LAGS), F32),
        in_specs=[VMEM] * 6,
        out_specs=pl.BlockSpec(memory_space=pl.ANY),
        scratch_shapes=[
            pltpu.VMEM((half, 128), F32),
            pltpu.VMEM((2, CHUNK, half, LAGS), F32),
            pltpu.SemaphoreType.DMA((2,)),
        ],
        compiler_params=pltpu.CompilerParams(vmem_limit_bytes=8 * 2**20),
    )(*args)

MESH = pl.DeviceIdType.MESH


def gather_kernel(mine_ref, first_ref, turn_ref, lag_first_ref, lag_turn_ref,
                  out_ref, table_ref, cos_ref, sin_ref, send_sems, recv_sems):
    s, r = lax.axis_index("src"), lax.axis_index("rcv")
    z, high = lax.div(s, 2), lax.rem(s, 2)
    low, y, core = lax.div(r, 8), lax.rem(lax.div(r, 2), 4), lax.rem(r, 2)

    def around(step):
        return (s, 8 * low + 2 * lax.rem(y + 4 + step, 4) + core)

    def along(step):
        return (2 * lax.rem(z + 8 + step, 8) + high, r)

    sibling = (s, 8 * low + 2 * y + 1 - core)
    beside = (s, 8 * (1 - low) + 2 * y + core)
    across = (2 * z + 1 - high, r)
    mirror = (r, s)

    def src_slot(step, other):
        column = 1 - low if other else low
        return core * 8 + column * 4 + lax.rem(y + 4 + step, 4)

    def rcv_slot(step, other):
        column = 1 - high if other else high
        return 16 + column * 8 + lax.rem(z + 8 + step, 8)

    peers = [sibling, beside, across, around(1), around(-1), along(1), along(-1)]
    barrier = pltpu.get_barrier_semaphore()
    for peer in peers:
        pl.semaphore_signal(barrier, inc=1, device_id=peer, device_id_type=MESH)

    @pl.when(s != r)
    def _():
        pl.semaphore_signal(barrier, inc=1, device_id=mirror, device_id_type=MESH)

    def copy(slot, device, source=None, sem=0):
        return pltpu.make_async_remote_copy(
            src_ref=out_ref.at[slot] if source is None else source,
            dst_ref=out_ref.at[slot], send_sem=send_sems.at[sem],
            recv_sem=recv_sems.at[slot], device_id=device, device_id_type=MESH)

    def arrive(slot):
        block = out_ref.at[slot]
        pltpu.make_async_copy(block, block, recv_sems.at[slot]).wait()

    own = src_slot(0, False)
    local = pltpu.make_async_copy(mine_ref, out_ref.at[own], recv_sems.at[own])
    local.start()
    width = 256
    blocks = iter(range(NF // width))

    def fill(count):
        for _ in range(count):
            block = next(blocks, None)
            if block is not None:
                fill_forward(first_ref, turn_ref, table_ref, block, width)

    pl.semaphore_wait(barrier, len(peers) + jnp.where(s == r, 0, 1))
    mirrored = copy(16 + lax.rem(r, 2) * 8 + lax.div(r, 2), mirror, mine_ref, 1)

    @pl.when(s != r)
    def _():
        mirrored.start()

    @pl.when(s == r)
    def _():
        slot = rcv_slot(0, False)
        pltpu.make_async_copy(mine_ref, out_ref.at[slot], recv_sems.at[slot]).start()

    for device in (beside, around(1), around(-1), sibling):
        copy(own, device, mine_ref).start()
    fill(1)
    arrive(rcv_slot(0, False))
    for device in (across, along(1), along(-1)):
        copy(rcv_slot(0, False), device).start()
    arrive(src_slot(0, True))
    for device in (around(1), around(-1), sibling):
        copy(src_slot(0, True), device).start()
    arrive(rcv_slot(0, True))
    for device in (along(1), along(-1)):
        copy(rcv_slot(0, True), device).start()
    fill(1)

    def pass_along(distance, last):
        for other in (False, True):
            for way in (1, -1):
                if last and (way == -1) != other:
                    continue
                slot = rcv_slot(-way * distance, other)
                arrive(slot)
                if distance < 3 or (distance == 3 and (way == -1) == other):
                    copy(slot, along(way)).start()

    for other in (False, True):
        for way in (1, -1):
            slot = src_slot(-way, other)
            arrive(slot)
            if (way == -1) == other:
                copy(slot, around(way)).start()
            copy(slot, sibling).start()
    pass_along(1, False)
    fill(1)
    for other in (False, True):
        slot = src_slot(2, other)
        arrive(slot)
        copy(slot, sibling).start()
    pass_along(2, False)
    fill(1)
    pass_along(3, False)
    fill(2)
    fill_lags(lag_first_ref, lag_turn_ref, cos_ref, sin_ref)
    for index in range(8):
        arrive((1 - core) * 8 + index)
    pass_along(4, True)
    local.wait()
    block = out_ref.at[pl.ds(0, 30)]
    pltpu.make_async_copy(block, block, send_sems.at[0]).wait()

    @pl.when(s != r)
    def _():
        mirrored.wait_send()


def gathered(mine, first, turn, lag_first, lag_turn):
    return pl.pallas_call(
        gather_kernel,
        out_shape=[
            jax.ShapeDtypeStruct((32,) + mine.shape, mine.dtype),
            jax.ShapeDtypeStruct((NS // 2, NS), BF16),
            jax.ShapeDtypeStruct((NF, LAGS // 2), BF16),
            jax.ShapeDtypeStruct((NF, LAGS // 2), BF16),
        ],
        in_specs=[VMEM] * 5,
        out_specs=[VMEM] * 4,
        scratch_shapes=[pltpu.SemaphoreType.DMA((2,)), pltpu.SemaphoreType.DMA((32,))],
        compiler_params=pltpu.CompilerParams(
            collective_id=0, has_side_effects=True, vmem_limit_bytes=16 * 2**20),
    )(mine, first, turn, lag_first, lag_turn)


def shards(traces, window_valid, pair_mask):
    marked = jnp.where(window_valid[:, :, None] != 0, traces, jnp.asarray(INVALID, traces.dtype))
    windows, channels, samples = traces.shape
    mine = marked.reshape(windows, channels, 2, samples // 2).transpose(2, 0, 1, 3)
    mine = mine.reshape(2 * windows * channels, samples // 2)
    first, turn, phase, lag_first, lag_turn = seeds()
    pieces, table, cos_table, sin_table = gathered(mine, first, turn, lag_first, lag_turn)
    src, rcv, flags = whitened(pieces, table, phase)
    return correlated(src, rcv, flags, pair_mask, cos_table, sin_table)


def solution(mesh):
    in_specs = (P(None, ("src", "rcv"), None), P(None, ("src", "rcv")), P("src", "rcv"))
    mapped = jax.shard_map(
        shards, mesh=mesh, in_specs=in_specs, out_specs=P("src", "rcv", None), check_vma=False)

    def run(traces, window_valid, pair_mask):
        with jax.sharding.use_abstract_mesh(mesh.abstract_mesh):
            return mapped(traces, window_valid, pair_mask)

    return run
```

```python
import functools
import math

import jax
import jax.numpy as jnp
import numpy as np
from jax import lax
from jax.experimental import pallas as pl
from jax.experimental.pallas import tpu as pltpu
from jax.sharding import PartitionSpec as P

NS = 3072
NF = 1536
LAGS = 512
HALF = 32
WIN = 2
EPSILON = 1e-06
STEP = 2.0 * math.pi / NS
INVALID = 100.0
F32 = jnp.float32
BF16 = jnp.bfloat16
VMEM = pl.BlockSpec(memory_space=pltpu.VMEM)


def cos_sin(angles):
    return np.stack([np.cos(angles), np.sin(angles)]).astype(np.float32)


def seeds():
    freqs = np.arange(1, NF + 1, dtype=np.float64) * STEP
    halves = np.arange(LAGS // 2, dtype=np.float64) + 0.5
    rows = np.zeros(32)
    rows[:16], rows[16:24], rows[24:] = np.arange(16), 16, 0.5
    lag_rows = np.full(24, 16 * STEP)
    lag_rows[:16] = freqs[:16]
    return cos_sin(rows[:, None] * freqs[None, :]), cos_sin(lag_rows[:, None] * halves[None, :])


def rotate(cosine, sine, turn_cos, turn_sin):
    return cosine * turn_cos - sine * turn_sin, sine * turn_cos + cosine * turn_sin


def fill_forward(seed, table, block, width):
    lanes = pl.ds(block * width, width)
    imag_lanes = pl.ds(NF + block * width, width)
    turn_cos, turn_sin = seed[0, 16:17, lanes], seed[1, 16:17, lanes]

    def rows(index, held):
        cosine, sine = held
        at = pl.ds(pl.multiple_of(index * 16, 16), 16)
        table[at, lanes] = cosine.astype(BF16)
        table[at, imag_lanes] = (-sine).astype(BF16)
        return rotate(cosine, sine, turn_cos, turn_sin)

    lax.fori_loop(0, NS // 32, rows, (seed[0, 0:16, lanes], seed[1, 0:16, lanes]))


def fill_lags(seed, cos_table, sin_table):
    turn_cos, turn_sin = seed[0, 16:17, :], seed[1, 16:17, :]

    def rows(index, held):
        cosine, sine = held
        at = pl.ds(pl.multiple_of(index * 16, 16), 16)
        cos_table[at, :] = cosine.astype(BF16)
        sin_table[at, :] = sine.astype(BF16)
        return rotate(cosine, sine, turn_cos, turn_sin)

    lax.fori_loop(0, NF // 16, rows, (seed[0, 0:16, :], seed[1, 0:16, :]))


def channel_group(slot):
    if slot < 16:
        core, low, y = slot // 8, slot // 4 % 2, slot % 4
        return 8 * low + 2 * y + core
    return slot % 8 * 2 + (slot - 16) // 8


def unpack(first_slot, count, pieces, flags_ref, ordered, left):
    for piece in range(count // 4):
        rows = pieces[first_slot + piece].astype(F32)
        first = 4 * channel_group(first_slot + piece)
        for part in range(4):
            ordered[part, first : first + 4, :] = rows[4 * part : 4 * part + 4]
    lane = lax.broadcasted_iota(jnp.int32, (count, 128), 1)
    flags = jnp.zeros((count, 128), F32)
    for window in range(WIN):
        valid = ordered[window, :, 0:1] < 0.5 * INVALID
        flags = jnp.where((lane == window) & valid, 1.0, flags)
        for part in (window, WIN + window):
            left[part * count : (part + 1) * count, :] = jnp.where(valid, ordered[part], 0.0).astype(BF16)
    flags_ref[...] = flags


def transform(block, left, table, spectrum, high, low):
    total = left.shape[0] // 2
    width = 256
    even = lax.broadcasted_iota(jnp.int32, (1, width), 1) % 2 == 0
    at = block * width
    square = None
    for base in (0, NF):
        lanes = slice(base + at, base + at + width)
        both = jnp.dot(left[...], table[:, lanes], preferred_element_type=F32)
        later = both[total:]
        value = both[:total] + jnp.where(even, -later, later)
        spectrum[:, lanes] = value
        square = value * value if square is None else square + value * value
    amplitude = jnp.sqrt(square)
    rounded = amplitude.astype(BF16)
    lanes = slice(128 + at, 128 + at + width)
    high[:, lanes] = rounded
    low[:, lanes] = (amplitude - rounded.astype(F32)).astype(BF16)


def pad(high, low):
    total = high.shape[0]
    for ref in (high, low):
        ref[:, 0:128] = jnp.zeros((total, 128), BF16)
        ref[:, 128 + NF : 256 + NF] = jnp.zeros((total, 128), BF16)


def band_table(width):
    offset = lax.broadcasted_iota(jnp.int32, (2 * width, width), 0) - lax.broadcasted_iota(
        jnp.int32, (2 * width, width), 1
    )
    return jnp.where((offset >= 128 - HALF) & (offset <= 128 + HALF), 1.0, 0.0).astype(BF16)


def smooth(block, spectrum, high, low, seed, src_ref, rcv_ref):
    width = 256
    band = band_table(width)
    at = block * width
    around = slice(at, at + 2 * width)
    running = jnp.dot(high[:, around], band, preferred_element_type=F32)
    running += jnp.dot(low[:, around], band, preferred_element_type=F32)
    factor = 1.0 / (running * (1.0 / (2 * HALF + 1)) + EPSILON)
    real_lanes = slice(at, at + width)
    imag_lanes = slice(NF + at, NF + at + width)
    real = (spectrum[:, real_lanes] * factor).astype(BF16)
    imag = (spectrum[:, imag_lanes] * factor).astype(BF16)
    half = real.shape[0] // WIN
    for window in range(WIN):
        rows = slice(window * half, window * half + half)
        if src_ref is not None:
            turn_cos, turn_sin = seed[0, 24:25, real_lanes], seed[1, 24:25, real_lanes]
            src_real, src_imag = real[rows].astype(F32), imag[rows].astype(F32)
            src_ref[window, :, real_lanes] = src_real * turn_cos + src_imag * turn_sin
            src_ref[window, :, imag_lanes] = src_imag * turn_cos - src_real * turn_sin
        else:
            rcv_ref[window, :, real_lanes] = real[rows]
            rcv_ref[window, :, imag_lanes] = imag[rows]


CHUNK = 8
WIDE = 256


def correlate_kernel(src_ref, rcv_ref, weights, cos_ref, sin_ref, out_ref, staged, out_sems):
    half = rcv_ref.shape[1]
    steps = half // CHUNK
    groups = half // 16
    blocks = NF // WIDE

    back = 127 - lax.broadcasted_iota(jnp.int32, (half, 128), 1)

    def finish(even_acc, odd_acc, near, source, slot):
        even, odd = pltpu.matmul_pop(even_acc), pltpu.matmul_pop(odd_acc)
        weight = jnp.broadcast_to(near[:, source : source + 1], (half, 128))
        width = LAGS // 2
        for block in range(width // 128):
            lanes = slice(block * 128, block * 128 + 128)
            e, o = even[:, lanes], odd[:, lanes]
            staged[slot, source, :, width + block * 128 : width + block * 128 + 128] = (e - o) * weight
            flipped = jnp.take_along_axis((e + o) * weight, back, axis=1)
            staged[slot, source, :, width - block * 128 - 128 : width - block * 128] = flipped

    def cross(eight, inside, block):
        real_rows, imag_rows = [], []
        halves = []
        for part in range(WIDE // 128):
            first = block * WIDE + part * 128
            lanes = (slice(first, first + 128), slice(NF + first, NF + first + 128))
            sent = [
                [
                    jnp.broadcast_to(src_ref[w, eight, inside : inside + 1, at], (16, 128)).astype(BF16)
                    for at in lanes
                ]
                for w in range(WIN)
            ]
            halves.append((lanes, sent))
        for g in range(groups):
            reals, imags = [], []
            for lanes, sent in halves:
                real = imag = None
                for w in range(WIN):
                    ar, ai = sent[w]
                    br, bi = (rcv_ref[w, 16 * g : 16 * g + 16, at] for at in lanes)
                    more_real = ar * br + ai * bi
                    more_imag = ai * br - ar * bi
                    real = more_real if real is None else real + more_real
                    imag = more_imag if imag is None else imag + more_imag
                reals.append(real)
                imags.append(imag)
            real_rows.append(jnp.concatenate(reals, axis=1))
            imag_rows.append(jnp.concatenate(imags, axis=1))
        return jnp.concatenate(real_rows, axis=0), jnp.concatenate(imag_rows, axis=0)

    def near_of(chunk):
        return pltpu.roll(weights[...], lax.rem(256 - chunk * CHUNK, 128), 1)

    def put(chunk):
        slot = chunk % 2 if isinstance(chunk, int) else lax.rem(chunk, 2)
        at = pl.ds(pl.multiple_of(chunk * CHUNK, CHUNK), CHUNK)
        return pltpu.make_async_copy(staged.at[slot], out_ref.at[at], out_sems.at[slot])

    def with_accumulators(even_accs, odd_accs):
        def do_chunk(chunk, now, finishing):
            near = near_of(chunk - 1)
            slot = 1 - now

            @pl.when(chunk >= 3)
            def _():
                put(chunk - 3).wait()

            done = 0
            for block in range(blocks):
                rows = pl.ds(block * WIDE, WIDE)
                pltpu.matmul_push_rhs(cos_ref[rows, :], block % 2, 0)
                pltpu.matmul_push_rhs(sin_ref[rows, :], block % 2, 1)
                for source in range(CHUNK):
                    if finishing and (block * CHUNK + source) * CHUNK >= done * blocks * CHUNK and done < CHUNK:
                        finish(even_accs[slot][done], odd_accs[slot][done], near, done, slot)
                        done += 1
                    real, imag = cross(chunk * (CHUNK // 8) + source // 8, source % 8, block)
                    load = block % 2 if source == 0 else None
                    pltpu.matmul_acc_lhs(even_accs[now][source], real, load_staged_rhs=load)
                    pltpu.matmul_acc_lhs(odd_accs[now][source], imag, load_staged_rhs=load)

            @pl.when(chunk >= 1)
            def _():
                put(chunk - 1).start()

        def step(pair, carry):
            do_chunk(2 * pair, 0, True)
            do_chunk(2 * pair + 1, 1, True)
            return carry

        zero = jnp.zeros((half, WIDE), BF16)
        for unit, (table, accs) in enumerate(((cos_ref, even_accs), (sin_ref, odd_accs))):
            pltpu.matmul_push_rhs(table[0:WIDE, :], 0, unit)
            for source in range(CHUNK):
                pltpu.matmul_acc_lhs(accs[1][source], zero, load_staged_rhs=0 if source == 0 else None)
        lax.fori_loop(0, steps // 2, step, 0)
        last = steps - 1
        put(last - 2).wait()
        near = near_of(last)
        for source in range(CHUNK):
            finish(even_accs[1][source], odd_accs[1][source], near, source, last % 2)
        put(last).start()
        put(last - 1).wait()
        put(last).wait()

    pl.run_scoped(
        with_accumulators,
        [[pltpu.ACC(0)((half, LAGS // 2), F32) for _ in range(CHUNK)] for _ in range(2)],
        [[pltpu.ACC(1)((half, LAGS // 2), F32) for _ in range(CHUNK)] for _ in range(2)],
    )


def correlated(src, rcv, weights, cos_table, sin_table):
    half = rcv.shape[1]
    args = (src.reshape(WIN, half // 8, 8, NS), rcv, weights, cos_table, sin_table)
    return pl.pallas_call(
        correlate_kernel,
        out_shape=jax.ShapeDtypeStruct((half, half, LAGS), F32),
        in_specs=[VMEM] * 5,
        out_specs=pl.BlockSpec(memory_space=pl.ANY),
        scratch_shapes=[
            pltpu.VMEM((2, CHUNK, half, LAGS), F32),
            pltpu.SemaphoreType.DMA((2,)),
        ],
        compiler_params=pltpu.CompilerParams(vmem_limit_bytes=8 * 2**20),
    )(*args)

MESH = pl.DeviceIdType.MESH


def spectra_kernel(traces_ref, valid_ref, seed_ref, lag_seed_ref, mask_ref,
                   src_ref, rcv_ref, weights_ref, cos_ref, sin_ref,
                   traces, valid, seed, lag_seed, mask, flags_ref, mine, pieces, table, ordered, left, spectrum, high, low_part,
                   local_sems, send_sems, recv_sems):
    s, r = lax.axis_index("src"), lax.axis_index("rcv")
    z, high_x = lax.div(s, 2), lax.rem(s, 2)
    low, y, core = lax.div(r, 8), lax.rem(lax.div(r, 2), 4), lax.rem(r, 2)

    def around(step):
        return (s, 8 * low + 2 * lax.rem(y + 4 + step, 4) + core)

    def along(step):
        return (2 * lax.rem(z + 8 + step, 8) + high_x, r)

    sibling = (s, 8 * low + 2 * y + 1 - core)
    beside = (s, 8 * (1 - low) + 2 * y + core)
    across = (2 * z + 1 - high_x, r)
    mirror = (r, s)

    def src_slot(step, other):
        column = 1 - low if other else low
        return core * 8 + column * 4 + lax.rem(y + 4 + step, 4)

    def rcv_slot(step, other):
        column = 1 - high_x if other else high_x
        return 16 + column * 8 + lax.rem(z + 8 + step, 8)

    loads = [
        pltpu.make_async_copy(source, target, local_sems.at[index])
        for index, (source, target) in enumerate(
            ((traces_ref, traces), (valid_ref, valid), (seed_ref, seed), (lag_seed_ref, lag_seed), (mask_ref, mask)))
    ]
    for load in loads:
        load.start()
    y_steps, z_steps = (1, -1, 2), (4, 3, -3, 2, -2, 1, -1)
    peers = [sibling, beside, across] + [around(k) for k in y_steps] + [along(k) for k in z_steps]
    barrier = pltpu.get_barrier_semaphore()
    for peer in peers:
        pl.semaphore_signal(barrier, inc=1, device_id=peer, device_id_type=MESH)

    @pl.when(s != r)
    def _():
        pl.semaphore_signal(barrier, inc=1, device_id=mirror, device_id_type=MESH)

    def copy(slot, device, source=None, sem=0):
        return pltpu.make_async_remote_copy(
            src_ref=pieces.at[slot] if source is None else source,
            dst_ref=pieces.at[slot], send_sem=send_sems.at[sem],
            recv_sem=recv_sems.at[slot], device_id=device, device_id_type=MESH)

    def arrive(slot):
        block = pieces.at[slot]
        pltpu.make_async_copy(block, block, recv_sems.at[slot]).wait()

    loads[0].wait()
    loads[1].wait()
    samples = NS // 2
    parts = []
    for window in range(WIN):
        rows = traces[window].astype(F32)
        keep = jnp.concatenate([valid[window : window + 1, c : c + 1] for c in range(rows.shape[0])], axis=0)
        parts.append(jnp.where(keep != 0, rows, INVALID))
    mine[...] = jnp.concatenate(
        [part[:, at : at + samples] for at in (0, samples) for part in parts], axis=0).astype(BF16)

    own = src_slot(0, False)
    local = pltpu.make_async_copy(mine, pieces.at[own], recv_sems.at[own])
    local.start()
    pl.semaphore_wait(barrier, len(peers) + jnp.where(s == r, 0, 1))
    mirrored = copy(16 + lax.rem(r, 2) * 8 + lax.div(r, 2), mirror, mine, 1)

    @pl.when(s != r)
    def _():
        mirrored.start()

    @pl.when(s == r)
    def _():
        slot = rcv_slot(0, False)
        pltpu.make_async_copy(mine, pieces.at[slot], recv_sems.at[slot]).start()

    for device in [beside] + [around(k) for k in y_steps] + [sibling]:
        copy(own, device, mine).start()
    loads[2].wait()
    loads[3].wait()
    width = 256
    blocks = NF // width
    filled = iter(range(blocks))

    def fill(count):
        for _ in range(count):
            fill_forward(seed, table, next(filled), width)

    def hand_over(steps):
        for step in steps:
            slot = rcv_slot(step, False)
            arrive(slot)
            copy(slot, across).start()

    fill(1)
    slot = rcv_slot(0, False)
    arrive(slot)
    for device in [along(k) for k in z_steps] + [across]:
        copy(slot, device).start()
    slot = src_slot(0, True)
    arrive(slot)
    for device in [around(k) for k in y_steps] + [sibling]:
        copy(slot, device).start()
    fill(2)
    for step in y_steps:
        slot = src_slot(step, False)
        arrive(slot)
        copy(slot, sibling).start()
    hand_over((1, -1))
    fill(1)
    for step in y_steps:
        slot = src_slot(step, True)
        arrive(slot)
        copy(slot, sibling).start()
    hand_over((2, -2))
    fill(2)
    fill_lags(lag_seed, cos_ref, sin_ref)
    pad(high, low_part)
    hand_over((3, -3))
    for index in range(8):
        arrive((1 - core) * 8 + index)
    local.wait()
    half = src_ref.shape[1]
    unpack(0, half, pieces, flags_ref.at[0:half], ordered, left)
    hand_over((4,))
    for block in range(blocks):
        transform(block, left, table, spectrum, high, low_part)
    for block in range(blocks):
        smooth(block, spectrum, high, low_part, seed, src_ref, None)
    for step in range(8):
        arrive(rcv_slot(step, True))
    unpack(16, half, pieces, flags_ref.at[half : 2 * half], ordered, left)
    loads[4].wait()
    flip = flags_ref[0:half, :].T
    counts = sum(flags_ref[half : 2 * half, w : w + 1] * flip[w : w + 1, :] for w in range(WIN))
    scale = mask[...].astype(F32).T * (1.0 / math.sqrt(NF)) / jnp.maximum(counts, 1.0)
    weights_ref[...] = jnp.concatenate([scale, jnp.zeros((half, 128 - half), F32)], axis=1)
    for block in range(blocks):
        transform(block, left, table, spectrum, high, low_part)
    for block in range(blocks):
        smooth(block, spectrum, high, low_part, seed, None, rcv_ref)
    block = pieces.at[pl.ds(0, 30)]
    pltpu.make_async_copy(block, block, send_sems.at[0]).wait()

    @pl.when(s != r)
    def _():
        mirrored.wait_send()


def spectra(half, traces, window_valid, pair_mask):
    seed, lag_seed = seeds()
    total = WIN * half
    far = pl.BlockSpec(memory_space=pltpu.HBM)
    rows = 2 * WIN * traces.shape[1]
    return pl.pallas_call(
        spectra_kernel,
        out_shape=[
            jax.ShapeDtypeStruct((WIN, half, NS), F32),
            jax.ShapeDtypeStruct((WIN, half, NS), BF16),
            jax.ShapeDtypeStruct((half, 128), F32),
            jax.ShapeDtypeStruct((NF, LAGS // 2), BF16),
            jax.ShapeDtypeStruct((NF, LAGS // 2), BF16),
        ],
        in_specs=[far] * 5,
        out_specs=[VMEM] * 5,
        scratch_shapes=[
            pltpu.VMEM(traces.shape, BF16),
            pltpu.VMEM(window_valid.shape, jnp.int32),
            pltpu.VMEM(seed.shape, F32),
            pltpu.VMEM(lag_seed.shape, F32),
            pltpu.VMEM(pair_mask.shape, jnp.int32),
            pltpu.VMEM((2 * half, 128), F32),
            pltpu.VMEM((rows, NS // 2), BF16),
            pltpu.VMEM((32, rows, NS // 2), BF16),
            pltpu.VMEM((NS // 2, NS), BF16),
            pltpu.VMEM((4, half, NS // 2), F32),
            pltpu.VMEM((2 * total, NS // 2), BF16),
            pltpu.VMEM((total, NS), F32),
            pltpu.VMEM((total, NF + 256), BF16),
            pltpu.VMEM((total, NF + 256), BF16),
            pltpu.SemaphoreType.DMA((5,)),
            pltpu.SemaphoreType.DMA((2,)),
            pltpu.SemaphoreType.DMA((32,)),
        ],
        compiler_params=pltpu.CompilerParams(
            collective_id=0, has_side_effects=True, vmem_limit_bytes=28 * 2**20),
    )(*(pltpu.with_memory_space_constraint(a, pltpu.HBM) for a in (traces, window_valid, jnp.asarray(seed), jnp.asarray(lag_seed), pair_mask)))


def shards(traces, window_valid, pair_mask):
    src, rcv, weights, cos_table, sin_table = spectra(pair_mask.shape[0], traces, window_valid, pair_mask)
    return correlated(src, rcv, weights, cos_table, sin_table)


def solution(mesh):
    in_specs = (P(None, ("src", "rcv"), None), P(None, ("src", "rcv")), P("src", "rcv"))
    mapped = jax.shard_map(
        shards, mesh=mesh, in_specs=in_specs, out_specs=P("src", "rcv", None), check_vma=False)

    def run(traces, window_valid, pair_mask):
        with jax.sharding.use_abstract_mesh(mesh.abstract_mesh):
            return mapped(traces, window_valid, pair_mask)

    return run
```

```python
import functools
import math

import jax
import jax.numpy as jnp
import numpy as np
from jax import lax
from jax.experimental import pallas as pl
from jax.experimental.pallas import tpu as pltpu
from jax.sharding import PartitionSpec as P

NS = 3072
NF = 1536
LAGS = 512
HALF = 32
WIN = 2
EPSILON = 1e-06
STEP = 2.0 * math.pi / NS
INVALID = 100.0
F32 = jnp.float32
BF16 = jnp.bfloat16
VMEM = pl.BlockSpec(memory_space=pltpu.VMEM)


def cos_sin(angles):
    return np.stack([np.cos(angles), np.sin(angles)]).astype(np.float32)


def seeds():
    freqs = np.arange(1, NF + 1, dtype=np.float64) * STEP
    halves = np.arange(LAGS // 2, dtype=np.float64) + 0.5
    rows = np.zeros(32)
    rows[:16], rows[16:24], rows[24:] = np.arange(16), 16, 0.5
    lag_rows = np.full(24, 16 * STEP)
    lag_rows[:16] = freqs[:16]
    return cos_sin(rows[:, None] * freqs[None, :]), cos_sin(lag_rows[:, None] * halves[None, :])


def rotate(cosine, sine, turn_cos, turn_sin):
    return cosine * turn_cos - sine * turn_sin, sine * turn_cos + cosine * turn_sin


def fill_forward(seed, table, block, width):
    lanes = pl.ds(block * width, width)
    imag_lanes = pl.ds(NF + block * width, width)
    turn_cos, turn_sin = seed[0, 16:17, lanes], seed[1, 16:17, lanes]

    def rows(index, held):
        cosine, sine = held
        at = pl.ds(pl.multiple_of(index * 16, 16), 16)
        table[at, lanes] = cosine.astype(BF16)
        table[at, imag_lanes] = (-sine).astype(BF16)
        return rotate(cosine, sine, turn_cos, turn_sin)

    lax.fori_loop(0, NS // 32, rows, (seed[0, 0:16, lanes], seed[1, 0:16, lanes]))


def fill_lags(seed, cos_table, sin_table):
    turn_cos, turn_sin = seed[0, 16:17, :], seed[1, 16:17, :]

    def rows(index, held):
        cosine, sine = held
        at = pl.ds(pl.multiple_of(index * 16, 16), 16)
        cos_table[at, :] = cosine.astype(BF16)
        sin_table[at, :] = sine.astype(BF16)
        return rotate(cosine, sine, turn_cos, turn_sin)

    lax.fori_loop(0, NF // 16, rows, (seed[0, 0:16, :], seed[1, 0:16, :]))


def channel_group(slot):
    core, low, y = slot // 8, slot // 4 % 2, slot % 4
    return 8 * low + 2 * y + core


def unpack(count, slot_of, row_of, pieces, ordered, left):
    for piece in range(count // 4):
        rows = pieces[slot_of(piece)].astype(F32)
        first = row_of(piece)
        for part in range(4):
            ordered[part, first : first + 4, :] = rows[4 * part : 4 * part + 4]
    lane = lax.broadcasted_iota(jnp.int32, (count, 128), 1)
    flags = jnp.zeros((count, 128), F32)
    for window in range(WIN):
        valid = ordered[window, 0:count, 0:1] < 0.5 * INVALID
        flags = jnp.where((lane == window) & valid, 1.0, flags)
        for part in (window, WIN + window):
            rows = jnp.where(valid, ordered[part, 0:count, :], 0.0)
            left[part * count : (part + 1) * count, :] = rows.astype(BF16)
    return flags


def transform(block, first, total, left, table, spectrum, high, low):
    width = 256
    even = lax.broadcasted_iota(jnp.int32, (1, width), 1) % 2 == 0
    at = block * width
    square = None
    rows = slice(first, first + total)
    for base in (0, NF):
        lanes = slice(base + at, base + at + width)
        both = jnp.dot(left[0 : 2 * total, :], table[:, lanes], preferred_element_type=F32)
        later = both[total:]
        value = both[:total] + jnp.where(even, -later, later)
        spectrum[rows, lanes] = value
        square = value * value if square is None else square + value * value
    amplitude = jnp.sqrt(square)
    rounded = amplitude.astype(BF16)
    lanes = slice(128 + at, 128 + at + width)
    high[rows, lanes] = rounded
    low[rows, lanes] = (amplitude - rounded.astype(F32)).astype(BF16)


def pad(high, low):
    total = high.shape[0]
    for ref in (high, low):
        ref[:, 0:128] = jnp.zeros((total, 128), BF16)
        ref[:, 128 + NF : 256 + NF] = jnp.zeros((total, 128), BF16)


def band_table(width):
    offset = lax.broadcasted_iota(jnp.int32, (2 * width, width), 0) - lax.broadcasted_iota(
        jnp.int32, (2 * width, width), 1
    )
    return jnp.where((offset >= 128 - HALF) & (offset <= 128 + HALF), 1.0, 0.0).astype(BF16)


def whiten(block, spectrum, high, low):
    width = 256
    band = band_table(width)
    at = block * width
    around = slice(at, at + 2 * width)
    running = jnp.dot(high[:, around], band, preferred_element_type=F32)
    running += jnp.dot(low[:, around], band, preferred_element_type=F32)
    factor = 1.0 / (running * (1.0 / (2 * HALF + 1)) + EPSILON)
    lanes = slice(at, at + width), slice(NF + at, NF + at + width)
    return lanes, [spectrum[:, part] * factor for part in lanes]


def put_sources(block, spectrum, high, low, seed, src_ref):
    (real_lanes, imag_lanes), parts = whiten(block, spectrum, high, low)
    real, imag = (part.astype(BF16).astype(F32) for part in parts)
    turn_cos, turn_sin = seed[0, 24:25, real_lanes], seed[1, 24:25, real_lanes]
    half = real.shape[0] // WIN
    for window in range(WIN):
        rows = slice(window * half, window * half + half)
        src_ref[window, :, real_lanes] = real[rows] * turn_cos + imag[rows] * turn_sin
        src_ref[window, :, imag_lanes] = imag[rows] * turn_cos - real[rows] * turn_sin


def interleave(own, other, high_x):
    rows, width = own.shape
    first = jnp.where(high_x == 0, own, other).reshape(rows // 8, 8, width)
    second = jnp.where(high_x == 0, other, own).reshape(rows // 8, 8, width)
    upper = lax.broadcasted_iota(jnp.int32, (1, 8, 1), 1) < 4
    even = jnp.where(upper, first, pltpu.roll(second, 4, 1))
    odd = jnp.where(upper, pltpu.roll(first, 4, 1), second)
    return jnp.stack([even, odd], axis=1).reshape(2 * rows, width)


def put_receivers(block, spectrum, high, low, high_x, rcv_ref):
    lanes, parts = whiten(block, spectrum, high, low)
    quarter = spectrum.shape[0] // 4
    for at, part in zip(lanes, parts):
        for window in range(WIN):
            own = part[window * quarter : (window + 1) * quarter]
            other = part[(2 + window) * quarter : (3 + window) * quarter]
            rcv_ref[window, :, at] = interleave(own, other, high_x).astype(BF16)


CHUNK = 8
WIDE = 256


def correlate_kernel(src_ref, rcv_ref, weights, cos_ref, sin_ref, out_ref, staged, out_sems):
    half = rcv_ref.shape[1]
    steps = half // CHUNK
    groups = half // 16
    blocks = NF // WIDE

    back = 127 - lax.broadcasted_iota(jnp.int32, (half, 128), 1)

    def finish(even_acc, odd_acc, near, source, slot):
        even, odd = pltpu.matmul_pop(even_acc), pltpu.matmul_pop(odd_acc)
        weight = jnp.broadcast_to(near[:, source : source + 1], (half, 128))
        width = LAGS // 2
        for block in range(width // 128):
            lanes = slice(block * 128, block * 128 + 128)
            e, o = even[:, lanes], odd[:, lanes]
            staged[slot, source, :, width + block * 128 : width + block * 128 + 128] = (e - o) * weight
            flipped = jnp.take_along_axis((e + o) * weight, back, axis=1)
            staged[slot, source, :, width - block * 128 - 128 : width - block * 128] = flipped

    def cross(eight, inside, block):
        real_rows, imag_rows = [], []
        halves = []
        for part in range(WIDE // 128):
            first = block * WIDE + part * 128
            lanes = (slice(first, first + 128), slice(NF + first, NF + first + 128))
            sent = [
                [
                    jnp.broadcast_to(src_ref[w, eight, inside : inside + 1, at], (16, 128)).astype(BF16)
                    for at in lanes
                ]
                for w in range(WIN)
            ]
            halves.append((lanes, sent))
        for g in range(groups):
            reals, imags = [], []
            for lanes, sent in halves:
                real = imag = None
                for w in range(WIN):
                    ar, ai = sent[w]
                    br, bi = (rcv_ref[w, 16 * g : 16 * g + 16, at] for at in lanes)
                    more_real = ar * br + ai * bi
                    more_imag = ai * br - ar * bi
                    real = more_real if real is None else real + more_real
                    imag = more_imag if imag is None else imag + more_imag
                reals.append(real)
                imags.append(imag)
            real_rows.append(jnp.concatenate(reals, axis=1))
            imag_rows.append(jnp.concatenate(imags, axis=1))
        return jnp.concatenate(real_rows, axis=0), jnp.concatenate(imag_rows, axis=0)

    def near_of(chunk):
        return pltpu.roll(weights[...], lax.rem(256 - chunk * CHUNK, 128), 1)

    def put(chunk):
        slot = chunk % 2 if isinstance(chunk, int) else lax.rem(chunk, 2)
        at = pl.ds(pl.multiple_of(chunk * CHUNK, CHUNK), CHUNK)
        return pltpu.make_async_copy(staged.at[slot], out_ref.at[at], out_sems.at[slot])

    def with_accumulators(even_accs, odd_accs):
        def do_chunk(chunk, now, finishing):
            near = near_of(chunk - 1)
            slot = 1 - now

            @pl.when(chunk >= 3)
            def _():
                put(chunk - 3).wait()

            done = 0
            for block in range(blocks):
                rows = pl.ds(block * WIDE, WIDE)
                pltpu.matmul_push_rhs(cos_ref[rows, :], block % 2, 0)
                pltpu.matmul_push_rhs(sin_ref[rows, :], block % 2, 1)
                for source in range(CHUNK):
                    if finishing and (block * CHUNK + source) * CHUNK >= done * blocks * CHUNK and done < CHUNK:
                        finish(even_accs[slot][done], odd_accs[slot][done], near, done, slot)
                        done += 1
                    real, imag = cross(chunk * (CHUNK // 8) + source // 8, source % 8, block)
                    load = block % 2 if source == 0 else None
                    pltpu.matmul_acc_lhs(even_accs[now][source], real, load_staged_rhs=load)
                    pltpu.matmul_acc_lhs(odd_accs[now][source], imag, load_staged_rhs=load)

            @pl.when(chunk >= 1)
            def _():
                put(chunk - 1).start()

        def step(pair, carry):
            do_chunk(2 * pair, 0, True)
            do_chunk(2 * pair + 1, 1, True)
            return carry

        zero = jnp.zeros((half, WIDE), BF16)
        for unit, (table, accs) in enumerate(((cos_ref, even_accs), (sin_ref, odd_accs))):
            pltpu.matmul_push_rhs(table[0:WIDE, :], 0, unit)
            for source in range(CHUNK):
                pltpu.matmul_acc_lhs(accs[1][source], zero, load_staged_rhs=0 if source == 0 else None)
        lax.fori_loop(0, steps // 2, step, 0)
        last = steps - 1
        put(last - 2).wait()
        near = near_of(last)
        for source in range(CHUNK):
            finish(even_accs[1][source], odd_accs[1][source], near, source, last % 2)
        put(last).start()
        put(last - 1).wait()
        put(last).wait()

    pl.run_scoped(
        with_accumulators,
        [[pltpu.ACC(0)((half, LAGS // 2), F32) for _ in range(CHUNK)] for _ in range(2)],
        [[pltpu.ACC(1)((half, LAGS // 2), F32) for _ in range(CHUNK)] for _ in range(2)],
    )


def correlated(src, rcv, weights, cos_table, sin_table):
    half = rcv.shape[1]
    args = (src.reshape(WIN, half // 8, 8, NS), rcv, weights, cos_table, sin_table)
    return pl.pallas_call(
        correlate_kernel,
        out_shape=jax.ShapeDtypeStruct((half, half, LAGS), F32),
        in_specs=[VMEM] * 5,
        out_specs=pl.BlockSpec(memory_space=pl.ANY),
        scratch_shapes=[
            pltpu.VMEM((2, CHUNK, half, LAGS), F32),
            pltpu.SemaphoreType.DMA((2,)),
        ],
        compiler_params=pltpu.CompilerParams(vmem_limit_bytes=8 * 2**20),
    )(*args)

MESH = pl.DeviceIdType.MESH


def spectra_kernel(traces_ref, valid_ref, seed_ref, lag_seed_ref, mask_ref,
                   src_ref, rcv_ref, weights_ref, cos_ref, sin_ref,
                   traces, valid, seed, lag_seed, mask, flags_ref, mine, pieces, table, ordered, left, spectrum, high, low_part,
                   local_sems, send_sems, recv_sems):
    s, r = lax.axis_index("src"), lax.axis_index("rcv")
    z, high_x = lax.div(s, 2), lax.rem(s, 2)
    low, y, core = lax.div(r, 8), lax.rem(lax.div(r, 2), 4), lax.rem(r, 2)

    def around(step):
        return (s, 8 * low + 2 * lax.rem(y + 4 + step, 4) + core)

    def along(step):
        return (2 * lax.rem(z + 8 + step, 8) + high_x, r)

    sibling = (s, 8 * low + 2 * y + 1 - core)
    beside = (s, 8 * (1 - low) + 2 * y + core)
    across = (2 * z + 1 - high_x, r)
    mirror = (r, s)

    def src_slot(step, other):
        column = 1 - low if other else low
        return core * 8 + column * 4 + lax.rem(y + 4 + step, 4)

    def rcv_slot(step, other):
        column = 1 - high_x if other else high_x
        return 16 + column * 8 + lax.rem(z + 8 + step, 8)

    loads = [
        pltpu.make_async_copy(source, target, local_sems.at[index])
        for index, (source, target) in enumerate(
            ((traces_ref, traces), (valid_ref, valid), (seed_ref, seed), (lag_seed_ref, lag_seed), (mask_ref, mask)))
    ]
    for load in loads:
        load.start()
    y_steps, z_steps = (1, -1, 2), (1, -1, 2, -2)
    way = 1 - 2 * core
    peers = [sibling, beside, across] + [around(k) for k in y_steps] + [along(k) for k in z_steps]
    barrier = pltpu.get_barrier_semaphore()
    for peer in peers:
        pl.semaphore_signal(barrier, inc=1, device_id=peer, device_id_type=MESH)

    @pl.when(s != r)
    def _():
        pl.semaphore_signal(barrier, inc=1, device_id=mirror, device_id_type=MESH)

    def copy(slot, device, source=None, sem=0):
        return pltpu.make_async_remote_copy(
            src_ref=pieces.at[slot] if source is None else source,
            dst_ref=pieces.at[slot], send_sem=send_sems.at[sem],
            recv_sem=recv_sems.at[slot], device_id=device, device_id_type=MESH)

    def arrive(slot):
        block = pieces.at[slot]
        pltpu.make_async_copy(block, block, recv_sems.at[slot]).wait()

    loads[0].wait()
    loads[1].wait()
    samples = NS // 2
    parts = []
    for window in range(WIN):
        rows = traces[window].astype(F32)
        keep = jnp.concatenate([valid[window : window + 1, c : c + 1] for c in range(rows.shape[0])], axis=0)
        parts.append(jnp.where(keep != 0, rows, INVALID))
    mine[...] = jnp.concatenate(
        [part[:, at : at + samples] for at in (0, samples) for part in parts], axis=0).astype(BF16)

    own = src_slot(0, False)
    local = pltpu.make_async_copy(mine, pieces.at[own], recv_sems.at[own])
    local.start()
    pl.semaphore_wait(barrier, len(peers) + jnp.where(s == r, 0, 1))
    mirrored = copy(16 + lax.rem(r, 2) * 8 + lax.div(r, 2), mirror, mine, 1)

    @pl.when(s != r)
    def _():
        mirrored.start()

    @pl.when(s == r)
    def _():
        slot = rcv_slot(0, False)
        pltpu.make_async_copy(mine, pieces.at[slot], recv_sems.at[slot]).start()

    for device in [beside] + [around(k) for k in y_steps] + [sibling]:
        copy(own, device, mine).start()
    loads[2].wait()
    loads[3].wait()
    width = 256
    blocks = NF // width
    filled = iter(range(blocks))

    def fill(count):
        for _ in range(count):
            fill_forward(seed, table, next(filled), width)

    def hand_over(steps):
        for step in steps:
            slot = rcv_slot(step, False)
            arrive(slot)
            copy(slot, across).start()

    fill(blocks)
    fill_lags(lag_seed, cos_ref, sin_ref)
    pad(high, low_part)
    slot = rcv_slot(0, False)
    arrive(slot)
    for device in [along(k) for k in z_steps] + [across]:
        copy(slot, device).start()
    slot = src_slot(0, True)
    arrive(slot)
    for device in [around(k) for k in y_steps] + [sibling]:
        copy(slot, device).start()
    for step in y_steps:
        slot = src_slot(step, False)
        arrive(slot)
        copy(slot, sibling).start()
    hand_over((1, -1))
    for step, onward in ((-2 * way, (2 * way, way)), (2 * way, (-way,))):
        slot = rcv_slot(step, False)
        arrive(slot)
        for further in onward:
            copy(slot, along(further)).start()
        copy(slot, across).start()
    for step in y_steps:
        slot = src_slot(step, True)
        arrive(slot)
        copy(slot, sibling).start()
    for index in range(8):
        arrive((1 - core) * 8 + index)
    local.wait()
    half = src_ref.shape[1]
    quarter = half // 2
    flags_ref[0:half, :] = unpack(
        half, lambda p: p, lambda p: 4 * channel_group(p), pieces, ordered, left)
    for block in range(blocks):
        transform(block, 0, 2 * half, left, table, spectrum, high, low_part)
        if block == 1:
            hand_over((3 * way, -3 * way))
        if block == 3:
            hand_over((4,))
    for block in range(blocks):
        put_sources(block, spectrum, high, low_part, seed, src_ref)
    flags = []
    for batch, column in enumerate((high_x, 1 - high_x)):
        if batch == 1:
            for step in range(8):
                arrive(rcv_slot(step, True))
        base = 16 + 8 * column
        flags.append(unpack(quarter, lambda p: base + p, lambda p: 4 * p, pieces, ordered, left))
        for block in range(blocks):
            transform(block, batch * half, half, left, table, spectrum, high, low_part)
    flags_ref[half : 2 * half, :] = interleave(flags[0], flags[1], high_x)
    loads[4].wait()
    flip = flags_ref[0:half, :].T
    counts = sum(flags_ref[half : 2 * half, w : w + 1] * flip[w : w + 1, :] for w in range(WIN))
    scale = mask[...].astype(F32).T * (1.0 / math.sqrt(NF)) / jnp.maximum(counts, 1.0)
    weights_ref[...] = jnp.concatenate([scale, jnp.zeros((half, 128 - half), F32)], axis=1)
    for block in range(blocks):
        put_receivers(block, spectrum, high, low_part, high_x, rcv_ref)
    block = pieces.at[pl.ds(0, 30)]
    pltpu.make_async_copy(block, block, send_sems.at[0]).wait()

    @pl.when(s != r)
    def _():
        mirrored.wait_send()


def spectra(half, traces, window_valid, pair_mask):
    seed, lag_seed = seeds()
    total = WIN * half
    far = pl.BlockSpec(memory_space=pltpu.HBM)
    rows = 2 * WIN * traces.shape[1]
    return pl.pallas_call(
        spectra_kernel,
        out_shape=[
            jax.ShapeDtypeStruct((WIN, half, NS), F32),
            jax.ShapeDtypeStruct((WIN, half, NS), BF16),
            jax.ShapeDtypeStruct((half, 128), F32),
            jax.ShapeDtypeStruct((NF, LAGS // 2), BF16),
            jax.ShapeDtypeStruct((NF, LAGS // 2), BF16),
        ],
        in_specs=[far] * 5,
        out_specs=[VMEM] * 5,
        scratch_shapes=[
            pltpu.VMEM(traces.shape, BF16),
            pltpu.VMEM(window_valid.shape, jnp.int32),
            pltpu.VMEM(seed.shape, F32),
            pltpu.VMEM(lag_seed.shape, F32),
            pltpu.VMEM(pair_mask.shape, jnp.int32),
            pltpu.VMEM((2 * half, 128), F32),
            pltpu.VMEM((rows, NS // 2), BF16),
            pltpu.VMEM((32, rows, NS // 2), BF16),
            pltpu.VMEM((NS // 2, NS), BF16),
            pltpu.VMEM((4, half, NS // 2), F32),
            pltpu.VMEM((2 * total, NS // 2), BF16),
            pltpu.VMEM((total, NS), F32),
            pltpu.VMEM((total, NF + 256), BF16),
            pltpu.VMEM((total, NF + 256), BF16),
            pltpu.SemaphoreType.DMA((5,)),
            pltpu.SemaphoreType.DMA((2,)),
            pltpu.SemaphoreType.DMA((32,)),
        ],
        compiler_params=pltpu.CompilerParams(
            collective_id=0, has_side_effects=True, vmem_limit_bytes=28 * 2**20),
    )(*(pltpu.with_memory_space_constraint(a, pltpu.HBM) for a in (traces, window_valid, jnp.asarray(seed), jnp.asarray(lag_seed), pair_mask)))


def shards(traces, window_valid, pair_mask):
    src, rcv, weights, cos_table, sin_table = spectra(pair_mask.shape[0], traces, window_valid, pair_mask)
    return correlated(src, rcv, weights, cos_table, sin_table)


def solution(mesh):
    in_specs = (P(None, ("src", "rcv"), None), P(None, ("src", "rcv")), P("src", "rcv"))
    mapped = jax.shard_map(
        shards, mesh=mesh, in_specs=in_specs, out_specs=P("src", "rcv", None), check_vma=False)

    def run(traces, window_valid, pair_mask):
        with jax.sharding.use_abstract_mesh(mesh.abstract_mesh):
            return mapped(traces, window_valid, pair_mask)

    return run
```

```python
import functools
import math

import jax
import jax.numpy as jnp
import numpy as np
from jax import lax
from jax.experimental import pallas as pl
from jax.experimental.pallas import tpu as pltpu
from jax.sharding import PartitionSpec as P

NS = 3072
NF = 1536
LAGS = 512
HALF = 32
WIN = 2
EPSILON = 1e-06
STEP = 2.0 * math.pi / NS
INVALID = 100.0
F32 = jnp.float32
BF16 = jnp.bfloat16
PARTS = 1
VMEM = pl.BlockSpec(memory_space=pltpu.VMEM)


def cos_sin(angles):
    return np.stack([np.cos(angles), np.sin(angles)]).astype(np.float32)


def seeds():
    freqs = np.arange(1, NF + 1, dtype=np.float64) * STEP
    halves = np.arange(LAGS // 2, dtype=np.float64) + 0.5
    rows = np.zeros(32)
    rows[:16], rows[16:24], rows[24:] = np.arange(16), 16, 0.5
    lag_rows = np.full(24, 16 * STEP)
    lag_rows[:16] = freqs[:16]
    return cos_sin(rows[:, None] * freqs[None, :]), cos_sin(lag_rows[:, None] * halves[None, :])


def rotate(cosine, sine, turn_cos, turn_sin):
    return cosine * turn_cos - sine * turn_sin, sine * turn_cos + cosine * turn_sin


def fill_forward(seed, table, block, width):
    lanes = pl.ds(block * width, width)
    imag_lanes = pl.ds(NF + block * width, width)
    turn_cos, turn_sin = seed[0, 16:17, lanes], seed[1, 16:17, lanes]

    def rows(index, held):
        cosine, sine = held
        at = pl.ds(pl.multiple_of(index * 16, 16), 16)
        table[at, lanes] = cosine.astype(BF16)
        table[at, imag_lanes] = (-sine).astype(BF16)
        return rotate(cosine, sine, turn_cos, turn_sin)

    lax.fori_loop(0, NS // 32, rows, (seed[0, 0:16, lanes], seed[1, 0:16, lanes]))


def fill_lags(seed, cos_table, sin_table):
    turn_cos, turn_sin = seed[0, 16:17, :], seed[1, 16:17, :]

    def rows(index, held):
        cosine, sine = held
        at = pl.ds(pl.multiple_of(index * 16, 16), 16)
        cos_table[at, :] = cosine.astype(BF16)
        sin_table[at, :] = sine.astype(BF16)
        return rotate(cosine, sine, turn_cos, turn_sin)

    lax.fori_loop(0, NF // 16, rows, (seed[0, 0:16, :], seed[1, 0:16, :]))


def channel_group(slot):
    core, low, y = slot // 8, slot // 4 % 2, slot % 4
    return 8 * low + 2 * y + core


def unpack(count, slot_of, row_of, pieces, ordered, left):
    for piece in range(count // 4):
        first = row_of(piece)
        width = NS // 2 // PARTS
        for index in range(PARTS):
            rows = pieces[slot_of(piece), index].astype(F32)
            lanes = slice(index * width, index * width + width)
            for part in range(4):
                ordered[part, first : first + 4, lanes] = rows[4 * part : 4 * part + 4]
    lane = lax.broadcasted_iota(jnp.int32, (count, 128), 1)
    flags = jnp.zeros((count, 128), F32)
    for window in range(WIN):
        valid = ordered[window, 0:count, 0:1] < 0.5 * INVALID
        flags = jnp.where((lane == window) & valid, 1.0, flags)
        for part in (window, WIN + window):
            rows = jnp.where(valid, ordered[part, 0:count, :], 0.0)
            left[part * count : (part + 1) * count, :] = rows.astype(BF16)
    return flags


def transform(block, first, total, left, table, spectrum, high, low):
    width = 256
    even = lax.broadcasted_iota(jnp.int32, (1, width), 1) % 2 == 0
    at = block * width
    square = None
    rows = slice(first, first + total)
    for base in (0, NF):
        lanes = slice(base + at, base + at + width)
        both = jnp.dot(left[0 : 2 * total, :], table[:, lanes], preferred_element_type=F32)
        later = both[total:]
        value = both[:total] + jnp.where(even, -later, later)
        spectrum[rows, lanes] = value
        square = value * value if square is None else square + value * value
    amplitude = jnp.sqrt(square)
    rounded = amplitude.astype(BF16)
    lanes = slice(128 + at, 128 + at + width)
    high[rows, lanes] = rounded
    low[rows, lanes] = (amplitude - rounded.astype(F32)).astype(BF16)


def pad(high, low):
    total = high.shape[0]
    for ref in (high, low):
        ref[:, 0:128] = jnp.zeros((total, 128), BF16)
        ref[:, 128 + NF : 256 + NF] = jnp.zeros((total, 128), BF16)


def band_table(width):
    offset = lax.broadcasted_iota(jnp.int32, (2 * width, width), 0) - lax.broadcasted_iota(
        jnp.int32, (2 * width, width), 1
    )
    return jnp.where((offset >= 128 - HALF) & (offset <= 128 + HALF), 1.0, 0.0).astype(BF16)


def whiten(block, spectrum, high, low):
    width = 256
    band = band_table(width)
    at = block * width
    around = slice(at, at + 2 * width)
    running = jnp.dot(high[:, around], band, preferred_element_type=F32)
    running += jnp.dot(low[:, around], band, preferred_element_type=F32)
    factor = 1.0 / (running * (1.0 / (2 * HALF + 1)) + EPSILON)
    lanes = slice(at, at + width), slice(NF + at, NF + at + width)
    return lanes, [spectrum[:, part] * factor for part in lanes]


def put_sources(block, spectrum, high, low, seed, src_ref):
    (real_lanes, imag_lanes), parts = whiten(block, spectrum, high, low)
    real, imag = (part.astype(BF16).astype(F32) for part in parts)
    turn_cos, turn_sin = seed[0, 24:25, real_lanes], seed[1, 24:25, real_lanes]
    half = real.shape[0] // WIN
    for window in range(WIN):
        rows = slice(window * half, window * half + half)
        src_ref[window, :, real_lanes] = real[rows] * turn_cos + imag[rows] * turn_sin
        src_ref[window, :, imag_lanes] = imag[rows] * turn_cos - real[rows] * turn_sin


def interleave(own, other, high_x):
    rows, width = own.shape
    first = jnp.where(high_x == 0, own, other).reshape(rows // 8, 8, width)
    second = jnp.where(high_x == 0, other, own).reshape(rows // 8, 8, width)
    upper = lax.broadcasted_iota(jnp.int32, (1, 8, 1), 1) < 4
    even = jnp.where(upper, first, pltpu.roll(second, 4, 1))
    odd = jnp.where(upper, pltpu.roll(first, 4, 1), second)
    return jnp.stack([even, odd], axis=1).reshape(2 * rows, width)


def put_receivers(block, spectrum, high, low, high_x, rcv_ref):
    lanes, parts = whiten(block, spectrum, high, low)
    quarter = spectrum.shape[0] // 4
    for at, part in zip(lanes, parts):
        for window in range(WIN):
            own = part[window * quarter : (window + 1) * quarter]
            other = part[(2 + window) * quarter : (3 + window) * quarter]
            rcv_ref[window, :, at] = interleave(own, other, high_x).astype(BF16)


CHUNK = 8
WIDE = 256


def correlate_kernel(src_ref, rcv_ref, weights, cos_ref, sin_ref, out_ref, staged, out_sems, last_sems):
    half = rcv_ref.shape[1]
    steps = half // CHUNK
    groups = half // 16
    blocks = NF // WIDE

    back = 127 - lax.broadcasted_iota(jnp.int32, (half, 128), 1)

    def finish(even_acc, odd_acc, near, source, slot):
        even, odd = pltpu.matmul_pop(even_acc), pltpu.matmul_pop(odd_acc)
        weight = jnp.broadcast_to(near[:, source : source + 1], (half, 128))
        width = LAGS // 2
        for block in range(width // 128):
            lanes = slice(block * 128, block * 128 + 128)
            e, o = even[:, lanes], odd[:, lanes]
            staged[slot, source, :, width + block * 128 : width + block * 128 + 128] = (e - o) * weight
            flipped = jnp.take_along_axis((e + o) * weight, back, axis=1)
            staged[slot, source, :, width - block * 128 - 128 : width - block * 128] = flipped

    def cross(eight, inside, block):
        real_rows, imag_rows = [], []
        halves = []
        for part in range(WIDE // 128):
            first = block * WIDE + part * 128
            lanes = (slice(first, first + 128), slice(NF + first, NF + first + 128))
            sent = [
                [
                    jnp.broadcast_to(src_ref[w, eight, inside : inside + 1, at], (16, 128)).astype(BF16)
                    for at in lanes
                ]
                for w in range(WIN)
            ]
            halves.append((lanes, sent))
        for g in range(groups):
            reals, imags = [], []
            for lanes, sent in halves:
                real = imag = None
                for w in range(WIN):
                    ar, ai = sent[w]
                    br, bi = (rcv_ref[w, 16 * g : 16 * g + 16, at] for at in lanes)
                    more_real = ar * br + ai * bi
                    more_imag = ai * br - ar * bi
                    real = more_real if real is None else real + more_real
                    imag = more_imag if imag is None else imag + more_imag
                reals.append(real)
                imags.append(imag)
            real_rows.append(jnp.concatenate(reals, axis=1))
            imag_rows.append(jnp.concatenate(imags, axis=1))
        return jnp.concatenate(real_rows, axis=0), jnp.concatenate(imag_rows, axis=0)

    def near_of(chunk):
        return pltpu.roll(weights[...], lax.rem(256 - chunk * CHUNK, 128), 1)

    def put(chunk):
        slot = chunk % 2 if isinstance(chunk, int) else lax.rem(chunk, 2)
        at = pl.ds(pl.multiple_of(chunk * CHUNK, CHUNK), CHUNK)
        return pltpu.make_async_copy(staged.at[slot], out_ref.at[at], out_sems.at[slot])

    def put_one(chunk, source):
        return pltpu.make_async_copy(
            staged.at[chunk % 2, source], out_ref.at[chunk * CHUNK + source], last_sems.at[source])

    def with_accumulators(even_accs, odd_accs):
        def do_chunk(chunk, now, finishing):
            near = near_of(chunk - 1)
            slot = 1 - now

            @pl.when(chunk >= 3)
            def _():
                put(chunk - 3).wait()

            done = 0
            for block in range(blocks):
                rows = pl.ds(block * WIDE, WIDE)
                pltpu.matmul_push_rhs(cos_ref[rows, :], block % 2, 0)
                pltpu.matmul_push_rhs(sin_ref[rows, :], block % 2, 1)
                for source in range(CHUNK):
                    if finishing and (block * CHUNK + source) * CHUNK >= done * blocks * CHUNK and done < CHUNK:
                        finish(even_accs[slot][done], odd_accs[slot][done], near, done, slot)
                        done += 1
                    real, imag = cross(chunk * (CHUNK // 8) + source // 8, source % 8, block)
                    load = block % 2 if source == 0 else None
                    pltpu.matmul_acc_lhs(even_accs[now][source], real, load_staged_rhs=load)
                    pltpu.matmul_acc_lhs(odd_accs[now][source], imag, load_staged_rhs=load)

            @pl.when(chunk >= 1)
            def _():
                put(chunk - 1).start()

        def step(pair, carry):
            do_chunk(2 * pair, 0, True)
            do_chunk(2 * pair + 1, 1, True)
            return carry

        lax.fori_loop(0, steps // 2, step, 0)
        last = steps - 1
        put(last - 2).wait()
        near = near_of(last)
        for source in range(CHUNK):
            finish(even_accs[1][source], odd_accs[1][source], near, source, last % 2)
            put_one(last, source).start()
        put(last - 1).wait()
        for source in range(CHUNK):
            put_one(last, source).wait()

    pl.run_scoped(
        with_accumulators,
        [[pltpu.ACC(0)((half, LAGS // 2), F32) for _ in range(CHUNK)] for _ in range(2)],
        [[pltpu.ACC(1)((half, LAGS // 2), F32) for _ in range(CHUNK)] for _ in range(2)],
    )


def correlated(src, rcv, weights, cos_table, sin_table):
    half = rcv.shape[1]
    args = (src.reshape(WIN, half // 8, 8, NS), rcv, weights, cos_table, sin_table)
    return pl.pallas_call(
        correlate_kernel,
        out_shape=jax.ShapeDtypeStruct((half, half, LAGS), F32),
        in_specs=[VMEM] * 5,
        out_specs=pl.BlockSpec(memory_space=pl.ANY),
        scratch_shapes=[
            pltpu.VMEM((2, CHUNK, half, LAGS), F32),
            pltpu.SemaphoreType.DMA((2,)),
            pltpu.SemaphoreType.DMA((CHUNK,)),
        ],
        compiler_params=pltpu.CompilerParams(vmem_limit_bytes=8 * 2**20),
    )(*args)

MESH = pl.DeviceIdType.MESH


def spectra_kernel(traces_ref, valid_ref, seed_ref, lag_seed_ref, mask_ref,
                   src_ref, rcv_ref, weights_ref, cos_ref, sin_ref,
                   traces, valid, seed, lag_seed, mask, flags_ref, mine, pieces, table, ordered, left, spectrum, high, low_part,
                   local_sems, send_sems, recv_sems):
    s, r = lax.axis_index("src"), lax.axis_index("rcv")
    z, high_x = lax.div(s, 2), lax.rem(s, 2)
    low, y, core = lax.div(r, 8), lax.rem(lax.div(r, 2), 4), lax.rem(r, 2)

    def around(step):
        return (s, 8 * low + 2 * lax.rem(y + 4 + step, 4) + core)

    def along(step):
        return (2 * lax.rem(z + 8 + step, 8) + high_x, r)

    sibling = (s, 8 * low + 2 * y + 1 - core)
    beside = (s, 8 * (1 - low) + 2 * y + core)
    across = (2 * z + 1 - high_x, r)
    mirror = (r, s)

    def src_slot(step, other):
        column = 1 - low if other else low
        return core * 8 + column * 4 + lax.rem(y + 4 + step, 4)

    def rcv_slot(step, other):
        column = 1 - high_x if other else high_x
        return 16 + column * 8 + lax.rem(z + 8 + step, 8)

    loads = [
        pltpu.make_async_copy(source, target, local_sems.at[index])
        for index, (source, target) in enumerate(
            ((traces_ref, traces), (valid_ref, valid), (seed_ref, seed), (lag_seed_ref, lag_seed), (mask_ref, mask)))
    ]
    for load in loads:
        load.start()
    y_steps, z_steps = (1, -1, 2), (2, -2, 1, -1)
    way = 1 - 2 * core
    def diagonal(step):
        return (2 * lax.rem(z + 8 + step, 8) + 1 - high_x, r)

    peers = [diagonal(-way), diagonal(way), diagonal(-2 * way)]
    peers += [sibling, beside, across] + [around(k) for k in y_steps] + [along(k) for k in z_steps]
    barrier = pltpu.get_barrier_semaphore()
    for peer in peers:
        pl.semaphore_signal(barrier, inc=1, device_id=peer, device_id_type=MESH)

    @pl.when(s != r)
    def _():
        pl.semaphore_signal(barrier, inc=1, device_id=mirror, device_id_type=MESH)

    def copy(slot, device, source=None, part=None, sem=0):
        target = pieces.at[slot] if part is None else pieces.at[slot, part]
        return pltpu.make_async_remote_copy(
            src_ref=target if source is None else source,
            dst_ref=target, send_sem=send_sems.at[sem],
            recv_sem=recv_sems.at[slot, part or 0], device_id=device, device_id_type=MESH)

    def arrive(slot, part=None):
        block = pieces.at[slot] if part is None else pieces.at[slot, part]
        pltpu.make_async_copy(block, block, recv_sems.at[slot, part or 0]).wait()

    loads[0].wait()
    loads[1].wait()
    samples = NS // 2
    parts = []
    for window in range(WIN):
        rows = traces[window].astype(F32)
        keep = jnp.concatenate([valid[window : window + 1, c : c + 1] for c in range(rows.shape[0])], axis=0)
        parts.append(jnp.where(keep != 0, rows, INVALID))
    width = samples // PARTS
    for index in range(PARTS):
        starts = [first + index * width for first in (0, samples)]
        mine[index] = jnp.concatenate(
            [part[:, at : at + width] for at in starts for part in parts], axis=0).astype(BF16)

    own = src_slot(0, False)
    local = pltpu.make_async_copy(mine, pieces.at[own], recv_sems.at[own, 0])
    local.start()
    pl.semaphore_wait(barrier, len(peers) + jnp.where(s == r, 0, 1))
    mirrored = [
        copy(16 + lax.rem(r, 2) * 8 + lax.div(r, 2), mirror, mine.at[part], part, 1 + part)
        for part in range(PARTS)
    ]

    @pl.when(s != r)
    def _():
        for part in range(PARTS):
            mirrored[part].start()

    @pl.when(s == r)
    def _():
        slot = rcv_slot(0, False)
        for part in range(PARTS):
            pltpu.make_async_copy(mine.at[part], pieces.at[slot, part], recv_sems.at[slot, part]).start()

    loads[2].wait()
    loads[3].wait()
    width = 256
    blocks = NF // width
    filled = iter(range(blocks))

    def fill(count):
        for _ in range(count):
            fill_forward(seed, table, next(filled), width)

    fill(2)
    for device in [beside] + [around(k) for k in y_steps] + [sibling]:
        copy(own, device, mine).start()
    fill(blocks - 2)
    fill_lags(lag_seed, cos_ref, sin_ref)
    pad(high, low_part)
    slot = rcv_slot(0, False)
    for part in range(PARTS):
        arrive(slot, part)
        for device in [along(k) for k in z_steps] + [across]:
            copy(slot, device, None, part).start()
    slot = src_slot(0, True)
    arrive(slot)
    for device in [around(k) for k in y_steps] + [sibling]:
        copy(slot, device).start()
    for part in range(PARTS):
        for step, onward in ((-2 * way, (2 * way, way)), (2 * way, (-way,))):
            slot = rcv_slot(step, False)
            arrive(slot, part)
            for further in onward:
                copy(slot, along(further), None, part).start()
                copy(slot, diagonal(further), None, part).start()
            copy(slot, across, None, part).start()
    slot = rcv_slot(0, True)
    for part in range(PARTS):
        arrive(slot, part)
        for device in (along(1), along(-1)):
            copy(slot, device, None, part).start()
    for step in y_steps:
        slot = src_slot(step, False)
        arrive(slot)
        copy(slot, sibling).start()
    for step in y_steps:
        slot = src_slot(step, True)
        arrive(slot)
        copy(slot, sibling).start()
    for index in range(8):
        arrive((1 - core) * 8 + index)
    local.wait()
    half = src_ref.shape[1]
    quarter = half // 2
    flags_ref[0:half, :] = unpack(
        half, lambda p: p, lambda p: 4 * channel_group(p), pieces, ordered, left)
    for block in range(blocks):
        transform(block, 0, 2 * half, left, table, spectrum, high, low_part)
    for block in range(blocks):
        put_sources(block, spectrum, high, low_part, seed, src_ref)
    flags = []
    for batch, column in enumerate((high_x, 1 - high_x)):
        for step in (1, 2, 3, 4, 5, 6, 7):
            if batch == 1 or step not in (2, 6):
                for part in range(PARTS):
                    arrive(rcv_slot(step, batch == 1), part)
        base = 16 + 8 * column
        flags.append(unpack(quarter, lambda p: base + p, lambda p: 4 * p, pieces, ordered, left))
        for block in range(blocks):
            transform(block, batch * half, half, left, table, spectrum, high, low_part)
    flags_ref[half : 2 * half, :] = interleave(flags[0], flags[1], high_x)
    loads[4].wait()
    flip = flags_ref[0:half, :].T
    counts = sum(flags_ref[half : 2 * half, w : w + 1] * flip[w : w + 1, :] for w in range(WIN))
    scale = mask[...].astype(F32).T * (1.0 / math.sqrt(NF)) / jnp.maximum(counts, 1.0)
    weights_ref[...] = jnp.concatenate([scale, jnp.zeros((half, 128 - half), F32)], axis=1)
    for block in range(blocks):
        put_receivers(block, spectrum, high, low_part, high_x, rcv_ref)
    block = pieces.at[pl.ds(0, 30)]
    pltpu.make_async_copy(block, block, send_sems.at[0]).wait()

    @pl.when(s != r)
    def _():
        for part in range(PARTS):
            mirrored[part].wait_send()


def spectra(half, traces, window_valid, pair_mask):
    seed, lag_seed = seeds()
    total = WIN * half
    far = pl.BlockSpec(memory_space=pltpu.HBM)
    rows = 2 * WIN * traces.shape[1]
    return pl.pallas_call(
        spectra_kernel,
        out_shape=[
            jax.ShapeDtypeStruct((WIN, half, NS), F32),
            jax.ShapeDtypeStruct((WIN, half, NS), BF16),
            jax.ShapeDtypeStruct((half, 128), F32),
            jax.ShapeDtypeStruct((NF, LAGS // 2), BF16),
            jax.ShapeDtypeStruct((NF, LAGS // 2), BF16),
        ],
        in_specs=[far] * 5,
        out_specs=[VMEM] * 5,
        scratch_shapes=[
            pltpu.VMEM(traces.shape, BF16),
            pltpu.VMEM(window_valid.shape, jnp.int32),
            pltpu.VMEM(seed.shape, F32),
            pltpu.VMEM(lag_seed.shape, F32),
            pltpu.VMEM(pair_mask.shape, jnp.int32),
            pltpu.VMEM((2 * half, 128), F32),
            pltpu.VMEM((PARTS, rows, NS // 2 // PARTS), BF16),
            pltpu.VMEM((32, PARTS, rows, NS // 2 // PARTS), BF16),
            pltpu.VMEM((NS // 2, NS), BF16),
            pltpu.VMEM((4, half, NS // 2), F32),
            pltpu.VMEM((2 * total, NS // 2), BF16),
            pltpu.VMEM((total, NS), F32),
            pltpu.VMEM((total, NF + 256), BF16),
            pltpu.VMEM((total, NF + 256), BF16),
            pltpu.SemaphoreType.DMA((5,)),
            pltpu.SemaphoreType.DMA((1 + PARTS,)),
            pltpu.SemaphoreType.DMA((32, PARTS)),
        ],
        compiler_params=pltpu.CompilerParams(
            collective_id=0, has_side_effects=True, vmem_limit_bytes=28 * 2**20),
    )(*(pltpu.with_memory_space_constraint(a, pltpu.HBM) for a in (traces, window_valid, jnp.asarray(seed), jnp.asarray(lag_seed), pair_mask)))


def shards(traces, window_valid, pair_mask):
    src, rcv, weights, cos_table, sin_table = spectra(pair_mask.shape[0], traces, window_valid, pair_mask)
    return correlated(src, rcv, weights, cos_table, sin_table)


def solution(mesh):
    in_specs = (P(None, ("src", "rcv"), None), P(None, ("src", "rcv")), P("src", "rcv"))
    mapped = jax.shard_map(
        shards, mesh=mesh, in_specs=in_specs, out_specs=P("src", "rcv", None), check_vma=False)

    def run(traces, window_valid, pair_mask):
        with jax.sharding.use_abstract_mesh(mesh.abstract_mesh):
            return mapped(traces, window_valid, pair_mask)

    return run
```

```python
import functools
import math

import jax
import jax.numpy as jnp
import numpy as np
from jax import lax
from jax.experimental import pallas as pl
from jax.experimental.pallas import tpu as pltpu
from jax.sharding import PartitionSpec as P

NS = 3072
NF = 1536
LAGS = 512
HALF = 32
WIN = 2
EPSILON = 1e-06
STEP = 2.0 * math.pi / NS
INVALID = 100.0
F32 = jnp.float32
BF16 = jnp.bfloat16
PARTS = 1
VMEM = pl.BlockSpec(memory_space=pltpu.VMEM)


def cos_sin(angles):
    return np.stack([np.cos(angles), np.sin(angles)]).astype(np.float32)


def seeds():
    freqs = np.arange(1, NF + 1, dtype=np.float64) * STEP
    halves = np.arange(LAGS // 2, dtype=np.float64) + 0.5
    rows = np.zeros(32)
    rows[:16], rows[16:24], rows[24:] = np.arange(16), 16, 0.5
    lag_rows = np.full(24, 16 * STEP)
    lag_rows[:16] = freqs[:16]
    return cos_sin(rows[:, None] * freqs[None, :]), cos_sin(lag_rows[:, None] * halves[None, :])


def rotate(cosine, sine, turn_cos, turn_sin):
    return cosine * turn_cos - sine * turn_sin, sine * turn_cos + cosine * turn_sin


def fill_forward(seed, table, block, width):
    lanes = pl.ds(block * width, width)
    imag_lanes = pl.ds(NF + block * width, width)
    turn_cos, turn_sin = seed[0, 16:17, lanes], seed[1, 16:17, lanes]

    def rows(index, held):
        cosine, sine = held
        at = pl.ds(pl.multiple_of(index * 16, 16), 16)
        table[at, lanes] = cosine.astype(BF16)
        table[at, imag_lanes] = (-sine).astype(BF16)
        return rotate(cosine, sine, turn_cos, turn_sin)

    lax.fori_loop(0, NS // 32, rows, (seed[0, 0:16, lanes], seed[1, 0:16, lanes]))


def fill_lags(seed, cos_table, sin_table):
    turn_cos, turn_sin = seed[0, 16:17, :], seed[1, 16:17, :]

    def rows(index, held):
        cosine, sine = held
        at = pl.ds(pl.multiple_of(index * 16, 16), 16)
        cos_table[at, :] = cosine.astype(BF16)
        sin_table[at, :] = sine.astype(BF16)
        return rotate(cosine, sine, turn_cos, turn_sin)

    lax.fori_loop(0, NF // 16, rows, (seed[0, 0:16, :], seed[1, 0:16, :]))


def channel_group(slot):
    core, low, y = slot // 8, slot // 4 % 2, slot % 4
    return 8 * low + 2 * y + core


def unpack(count, slot_of, row_of, pieces, ordered, left):
    for piece in range(count // 4):
        first = row_of(piece)
        width = NS // 2 // PARTS
        for index in range(PARTS):
            rows = pieces[slot_of(piece), index].astype(F32)
            lanes = slice(index * width, index * width + width)
            for part in range(4):
                ordered[part, first : first + 4, lanes] = rows[4 * part : 4 * part + 4]
    lane = lax.broadcasted_iota(jnp.int32, (count, 128), 1)
    flags = jnp.zeros((count, 128), F32)
    for window in range(WIN):
        valid = ordered[window, 0:count, 0:1] < 0.5 * INVALID
        flags = jnp.where((lane == window) & valid, 1.0, flags)
        for part in (window, WIN + window):
            rows = jnp.where(valid, ordered[part, 0:count, :], 0.0)
            left[part * count : (part + 1) * count, :] = rows.astype(BF16)
    return flags


def transform(block, left, table, spectrum, high, low):
    width = 256
    even = lax.broadcasted_iota(jnp.int32, (1, width), 1) % 2 == 0
    at = block * width
    square = None
    total = spectrum.shape[0]
    for base in (0, NF):
        lanes = slice(base + at, base + at + width)
        both = jnp.dot(left[0 : 2 * total, :], table[:, lanes], preferred_element_type=F32)
        later = both[total:]
        value = both[:total] + jnp.where(even, -later, later)
        spectrum[:, lanes] = value
        square = value * value if square is None else square + value * value
    amplitude = jnp.sqrt(square)
    rounded = amplitude.astype(BF16)
    lanes = slice(128 + at, 128 + at + width)
    high[:, lanes] = rounded
    low[:, lanes] = (amplitude - rounded.astype(F32)).astype(BF16)


def pad(high, low):
    total = high.shape[0]
    for ref in (high, low):
        ref[:, 0:128] = jnp.zeros((total, 128), BF16)
        ref[:, 128 + NF : 256 + NF] = jnp.zeros((total, 128), BF16)


def band_table(width):
    offset = lax.broadcasted_iota(jnp.int32, (2 * width, width), 0) - lax.broadcasted_iota(
        jnp.int32, (2 * width, width), 1
    )
    return jnp.where((offset >= 128 - HALF) & (offset <= 128 + HALF), 1.0, 0.0).astype(BF16)


def whiten(block, spectrum, high, low):
    width = 256
    band = band_table(width)
    at = block * width
    around = slice(at, at + 2 * width)
    running = jnp.dot(high[:, around], band, preferred_element_type=F32)
    running += jnp.dot(low[:, around], band, preferred_element_type=F32)
    factor = 1.0 / (running * (1.0 / (2 * HALF + 1)) + EPSILON)
    lanes = slice(at, at + width), slice(NF + at, NF + at + width)
    return lanes, [spectrum[:, part] * factor for part in lanes]


def put_sources(block, spectrum, high, low, seed, src_ref):
    (real_lanes, imag_lanes), parts = whiten(block, spectrum, high, low)
    real, imag = (part.astype(BF16).astype(F32) for part in parts)
    turn_cos, turn_sin = seed[0, 24:25, real_lanes], seed[1, 24:25, real_lanes]
    half = real.shape[0] // WIN
    for window in range(WIN):
        rows = slice(window * half, window * half + half)
        src_ref[window, :, real_lanes] = real[rows] * turn_cos + imag[rows] * turn_sin
        src_ref[window, :, imag_lanes] = imag[rows] * turn_cos - real[rows] * turn_sin


def put_receivers(block, spectrum, high, low, first, rcv_ref):
    lanes, parts = whiten(block, spectrum, high, low)
    count = spectrum.shape[0] // WIN
    rows = pl.ds(pl.multiple_of(first, count), count)
    for at, part in zip(lanes, parts):
        for window in range(WIN):
            rcv_ref[window, rows, at] = part[window * count : (window + 1) * count].astype(BF16)


CHUNK = 8
WIDE = 256


def correlate_kernel(src_ref, rcv_ref, weights, cos_ref, sin_ref, out_ref, staged, out_sems, last_sems):
    half = rcv_ref.shape[1]
    steps = half // CHUNK
    groups = half // 16
    blocks = NF // WIDE

    back = 127 - lax.broadcasted_iota(jnp.int32, (half, 128), 1)

    def finish(even_acc, odd_acc, near, source, slot):
        even, odd = pltpu.matmul_pop(even_acc), pltpu.matmul_pop(odd_acc)
        weight = jnp.broadcast_to(near[:, source : source + 1], (half, 128))
        width = LAGS // 2
        for block in range(width // 128):
            lanes = slice(block * 128, block * 128 + 128)
            e, o = even[:, lanes], odd[:, lanes]
            staged[slot, source, :, width + block * 128 : width + block * 128 + 128] = (e - o) * weight
            flipped = jnp.take_along_axis((e + o) * weight, back, axis=1)
            staged[slot, source, :, width - block * 128 - 128 : width - block * 128] = flipped

    def cross(eight, inside, block):
        real_rows, imag_rows = [], []
        halves = []
        for part in range(WIDE // 128):
            first = block * WIDE + part * 128
            lanes = (slice(first, first + 128), slice(NF + first, NF + first + 128))
            sent = [
                [
                    jnp.broadcast_to(src_ref[w, eight, inside : inside + 1, at], (16, 128)).astype(BF16)
                    for at in lanes
                ]
                for w in range(WIN)
            ]
            halves.append((lanes, sent))
        for g in range(groups):
            reals, imags = [], []
            for lanes, sent in halves:
                real = imag = None
                for w in range(WIN):
                    ar, ai = sent[w]
                    br, bi = (rcv_ref[w, 16 * g : 16 * g + 16, at] for at in lanes)
                    more_real = ar * br + ai * bi
                    more_imag = ai * br - ar * bi
                    real = more_real if real is None else real + more_real
                    imag = more_imag if imag is None else imag + more_imag
                reals.append(real)
                imags.append(imag)
            real_rows.append(jnp.concatenate(reals, axis=1))
            imag_rows.append(jnp.concatenate(imags, axis=1))
        return jnp.concatenate(real_rows, axis=0), jnp.concatenate(imag_rows, axis=0)

    def near_of(chunk):
        return pltpu.roll(weights[...], lax.rem(256 - chunk * CHUNK, 128), 1)

    def put(chunk):
        slot = chunk % 2 if isinstance(chunk, int) else lax.rem(chunk, 2)
        at = pl.ds(pl.multiple_of(chunk * CHUNK, CHUNK), CHUNK)
        return pltpu.make_async_copy(staged.at[slot], out_ref.at[at], out_sems.at[slot])

    def put_one(chunk, source):
        return pltpu.make_async_copy(
            staged.at[chunk % 2, source], out_ref.at[chunk * CHUNK + source], last_sems.at[source])

    def with_accumulators(even_accs, odd_accs):
        def do_chunk(chunk, now, finishing):
            near = near_of(chunk - 1)
            slot = 1 - now

            @pl.when(chunk >= 3)
            def _():
                put(chunk - 3).wait()

            done = 0
            for block in range(blocks):
                rows = pl.ds(block * WIDE, WIDE)
                pltpu.matmul_push_rhs(cos_ref[rows, :], block % 2, 0)
                pltpu.matmul_push_rhs(sin_ref[rows, :], block % 2, 1)
                for source in range(CHUNK):
                    if finishing and (block * CHUNK + source) * CHUNK >= done * blocks * CHUNK and done < CHUNK:
                        finish(even_accs[slot][done], odd_accs[slot][done], near, done, slot)
                        done += 1
                    real, imag = cross(chunk * (CHUNK // 8) + source // 8, source % 8, block)
                    load = block % 2 if source == 0 else None
                    pltpu.matmul_acc_lhs(even_accs[now][source], real, load_staged_rhs=load)
                    pltpu.matmul_acc_lhs(odd_accs[now][source], imag, load_staged_rhs=load)

            @pl.when(chunk >= 1)
            def _():
                put(chunk - 1).start()

        def step(pair, carry):
            do_chunk(2 * pair, 0, True)
            do_chunk(2 * pair + 1, 1, True)
            return carry

        lax.fori_loop(0, steps // 2, step, 0)
        last = steps - 1
        put(last - 2).wait()
        near = near_of(last)
        for source in range(CHUNK):
            finish(even_accs[1][source], odd_accs[1][source], near, source, last % 2)
            put_one(last, source).start()
        put(last - 1).wait()
        for source in range(CHUNK):
            put_one(last, source).wait()

    pl.run_scoped(
        with_accumulators,
        [[pltpu.ACC(0)((half, LAGS // 2), F32) for _ in range(CHUNK)] for _ in range(2)],
        [[pltpu.ACC(1)((half, LAGS // 2), F32) for _ in range(CHUNK)] for _ in range(2)],
    )


def correlated(src, rcv, weights, cos_table, sin_table):
    half = rcv.shape[1]
    args = (src.reshape(WIN, half // 8, 8, NS), rcv, weights, cos_table, sin_table)
    return pl.pallas_call(
        correlate_kernel,
        out_shape=jax.ShapeDtypeStruct((half, half, LAGS), F32),
        in_specs=[VMEM] * 5,
        out_specs=pl.BlockSpec(memory_space=pl.ANY),
        scratch_shapes=[
            pltpu.VMEM((2, CHUNK, half, LAGS), F32),
            pltpu.SemaphoreType.DMA((2,)),
            pltpu.SemaphoreType.DMA((CHUNK,)),
        ],
        compiler_params=pltpu.CompilerParams(vmem_limit_bytes=8 * 2**20),
    )(*args)

MESH = pl.DeviceIdType.MESH


def spectra_kernel(traces_ref, valid_ref, seed_ref, lag_seed_ref, mask_ref,
                   src_ref, rcv_ref, weights_ref, cos_ref, sin_ref,
                   traces, valid, seed, lag_seed, mask, flags_ref, mine, pieces, table, ordered, left, spectrum, high, low_part,
                   local_sems, send_sems, recv_sems):
    s, r = lax.axis_index("src"), lax.axis_index("rcv")
    z, high_x = lax.div(s, 2), lax.rem(s, 2)
    low, y, core = lax.div(r, 8), lax.rem(lax.div(r, 2), 4), lax.rem(r, 2)

    def around(step):
        return (s, 8 * low + 2 * lax.rem(y + 4 + step, 4) + core)

    def along(step):
        return (2 * lax.rem(z + 8 + step, 8) + high_x, r)

    sibling = (s, 8 * low + 2 * y + 1 - core)
    beside = (s, 8 * (1 - low) + 2 * y + core)
    across = (2 * z + 1 - high_x, r)
    own_low = lax.rem(low + high_x + core, 2)
    mirror_x = lax.rem(high_x + low + lax.div(z, 4), 2)
    mirror = (2 * lax.rem(r, 8) + mirror_x, s)
    mirrored_from = (r, 8 * own_low + z)
    away = jnp.logical_or(mirror[0] != s, s != r)

    def src_slot(step, other):
        column = 1 - low if other else low
        return core * 8 + column * 4 + lax.rem(y + 4 + step, 4)

    def rcv_slot(step, other):
        column = 1 - own_low if other else own_low
        return 16 + column * 8 + lax.rem(z + 8 + step, 8)

    loads = [
        pltpu.make_async_copy(source, target, local_sems.at[index])
        for index, (source, target) in enumerate(
            ((traces_ref, traces), (valid_ref, valid), (seed_ref, seed), (lag_seed_ref, lag_seed), (mask_ref, mask)))
    ]
    for load in loads:
        load.start()
    y_steps, z_steps = (1, -1, 2), (2, -2, 1, -1)
    way = 1 - 2 * core
    def diagonal(step):
        return (2 * lax.rem(z + 8 + step, 8) + 1 - high_x, r)

    peers = [diagonal(-way), diagonal(way), diagonal(-2 * way)]
    peers += [sibling, beside, across] + [around(k) for k in y_steps] + [along(k) for k in z_steps]
    barrier = pltpu.get_barrier_semaphore()
    for peer in peers:
        pl.semaphore_signal(barrier, inc=1, device_id=peer, device_id_type=MESH)

    @pl.when(away)
    def _():
        pl.semaphore_signal(barrier, inc=1, device_id=mirrored_from, device_id_type=MESH)

    def copy(slot, device, source=None, part=None, sem=0):
        target = pieces.at[slot] if part is None else pieces.at[slot, part]
        return pltpu.make_async_remote_copy(
            src_ref=target if source is None else source,
            dst_ref=target, send_sem=send_sems.at[sem],
            recv_sem=recv_sems.at[slot, part or 0], device_id=device, device_id_type=MESH)

    def arrive(slot, part=None):
        block = pieces.at[slot] if part is None else pieces.at[slot, part]
        pltpu.make_async_copy(block, block, recv_sems.at[slot, part or 0]).wait()

    loads[0].wait()
    loads[1].wait()
    samples = NS // 2
    parts = []
    for window in range(WIN):
        rows = traces[window].astype(F32)
        keep = jnp.concatenate([valid[window : window + 1, c : c + 1] for c in range(rows.shape[0])], axis=0)
        parts.append(jnp.where(keep != 0, rows, INVALID))
    width = samples // PARTS
    for index in range(PARTS):
        starts = [first + index * width for first in (0, samples)]
        mine[index] = jnp.concatenate(
            [part[:, at : at + width] for at in starts for part in parts], axis=0).astype(BF16)

    own = src_slot(0, False)
    local = pltpu.make_async_copy(mine, pieces.at[own], recv_sems.at[own, 0])
    local.start()
    pl.semaphore_wait(barrier, len(peers) + jnp.where(away, 1, 0))
    mirrored = [
        copy(16 + r, mirror, mine.at[part], part, 1 + part)
        for part in range(PARTS)
    ]

    @pl.when(away)
    def _():
        for part in range(PARTS):
            mirrored[part].start()

    @pl.when(jnp.logical_not(away))
    def _():
        slot = rcv_slot(0, False)
        for part in range(PARTS):
            pltpu.make_async_copy(mine.at[part], pieces.at[slot, part], recv_sems.at[slot, part]).start()

    loads[2].wait()
    loads[3].wait()
    width = 256
    blocks = NF // width
    filled = iter(range(blocks))

    def fill(count):
        for _ in range(count):
            fill_forward(seed, table, next(filled), width)

    fill(2)
    for device in [beside] + [around(k) for k in y_steps] + [sibling]:
        copy(own, device, mine).start()
    fill(blocks - 2)
    fill_lags(lag_seed, cos_ref, sin_ref)
    pad(high, low_part)
    slot = rcv_slot(0, False)
    for part in range(PARTS):
        arrive(slot, part)
        for device in [along(k) for k in z_steps] + [across]:
            copy(slot, device, None, part).start()
    slot = src_slot(0, True)
    arrive(slot)
    for device in [around(k) for k in y_steps] + [sibling]:
        copy(slot, device).start()
    for part in range(PARTS):
        for step, onward in ((-2 * way, (2 * way, way)), (2 * way, (-way,))):
            slot = rcv_slot(step, False)
            arrive(slot, part)
            for further in onward:
                copy(slot, along(further), None, part).start()
                copy(slot, diagonal(further), None, part).start()
            copy(slot, across, None, part).start()
    slot = rcv_slot(0, True)
    for part in range(PARTS):
        arrive(slot, part)
        for device in (along(1), along(-1)):
            copy(slot, device, None, part).start()
    for step in y_steps:
        slot = src_slot(step, False)
        arrive(slot)
        copy(slot, sibling).start()
    for step in y_steps:
        slot = src_slot(step, True)
        arrive(slot)
        copy(slot, sibling).start()
    for index in range(8):
        arrive((1 - core) * 8 + index)
    local.wait()
    half = src_ref.shape[1]
    quarter = half // 2
    flags_ref[0:half, :] = unpack(
        half, lambda p: p, lambda p: 4 * channel_group(p), pieces, ordered, left)
    for block in range(blocks):
        transform(block, left, table, spectrum, high, low_part)
    for block in range(blocks):
        put_sources(block, spectrum, high, low_part, seed, src_ref)
    views = [ref.at[0:half] for ref in (spectrum, high, low_part)]
    for batch, column in enumerate((own_low, 1 - own_low)):
        for step in range(8):
            if step not in ((0, 2, 6), (0,))[batch]:
                arrive(rcv_slot(step, batch == 1), 0)
        base = 16 + 8 * column
        first = quarter * column
        flags_ref[pl.ds(pl.multiple_of(half + first, quarter), quarter), :] = unpack(
            quarter, lambda p: base + p, lambda p: 4 * p, pieces, ordered, left)
        for block in range(blocks):
            transform(block, left, table, *views)
        for block in range(blocks):
            put_receivers(block, *views, first, rcv_ref)
    loads[4].wait()
    flip = flags_ref[0:half, :].T
    counts = sum(flags_ref[half : 2 * half, w : w + 1] * flip[w : w + 1, :] for w in range(WIN))
    scale = mask[...].astype(F32).T * (1.0 / math.sqrt(NF)) / jnp.maximum(counts, 1.0)
    weights_ref[...] = jnp.concatenate([scale, jnp.zeros((half, 128 - half), F32)], axis=1)
    block = pieces.at[pl.ds(0, 30)]
    pltpu.make_async_copy(block, block, send_sems.at[0]).wait()

    @pl.when(away)
    def _():
        for part in range(PARTS):
            mirrored[part].wait_send()


def spectra(half, traces, window_valid, pair_mask):
    seed, lag_seed = seeds()
    total = WIN * half
    far = pl.BlockSpec(memory_space=pltpu.HBM)
    rows = 2 * WIN * traces.shape[1]
    return pl.pallas_call(
        spectra_kernel,
        out_shape=[
            jax.ShapeDtypeStruct((WIN, half, NS), F32),
            jax.ShapeDtypeStruct((WIN, half, NS), BF16),
            jax.ShapeDtypeStruct((half, 128), F32),
            jax.ShapeDtypeStruct((NF, LAGS // 2), BF16),
            jax.ShapeDtypeStruct((NF, LAGS // 2), BF16),
        ],
        in_specs=[far] * 5,
        out_specs=[VMEM] * 5,
        scratch_shapes=[
            pltpu.VMEM(traces.shape, BF16),
            pltpu.VMEM(window_valid.shape, jnp.int32),
            pltpu.VMEM(seed.shape, F32),
            pltpu.VMEM(lag_seed.shape, F32),
            pltpu.VMEM(pair_mask.shape, jnp.int32),
            pltpu.VMEM((2 * half, 128), F32),
            pltpu.VMEM((PARTS, rows, NS // 2 // PARTS), BF16),
            pltpu.VMEM((32, PARTS, rows, NS // 2 // PARTS), BF16),
            pltpu.VMEM((NS // 2, NS), BF16),
            pltpu.VMEM((4, half, NS // 2), F32),
            pltpu.VMEM((2 * total, NS // 2), BF16),
            pltpu.VMEM((total, NS), F32),
            pltpu.VMEM((total, NF + 256), BF16),
            pltpu.VMEM((total, NF + 256), BF16),
            pltpu.SemaphoreType.DMA((5,)),
            pltpu.SemaphoreType.DMA((1 + PARTS,)),
            pltpu.SemaphoreType.DMA((32, PARTS)),
        ],
        compiler_params=pltpu.CompilerParams(
            collective_id=0, has_side_effects=True, vmem_limit_bytes=28 * 2**20),
    )(*(pltpu.with_memory_space_constraint(a, pltpu.HBM) for a in (traces, window_valid, jnp.asarray(seed), jnp.asarray(lag_seed), pair_mask)))


def shards(traces, window_valid, pair_mask):
    src, rcv, weights, cos_table, sin_table = spectra(pair_mask.shape[0], traces, window_valid, pair_mask)
    return correlated(src, rcv, weights, cos_table, sin_table)


def solution(mesh):
    in_specs = (P(None, ("src", "rcv"), None), P(None, ("src", "rcv")), P("src", "rcv"))
    mapped = jax.shard_map(
        shards, mesh=mesh, in_specs=in_specs, out_specs=P("src", "rcv", None), check_vma=False)

    def run(traces, window_valid, pair_mask):
        with jax.sharding.use_abstract_mesh(mesh.abstract_mesh):
            return mapped(traces, window_valid, pair_mask)

    return run
```

```python
import functools
import math

import jax
import jax.numpy as jnp
import numpy as np
from jax import lax
from jax.experimental import pallas as pl
from jax.experimental.pallas import tpu as pltpu
from jax.sharding import PartitionSpec as P

NS = 3072
NF = 1536
LAGS = 512
HALF = 32
WIN = 2
EPSILON = 1e-06
STEP = 2.0 * math.pi / NS
F32 = jnp.float32
BF16 = jnp.bfloat16
VMEM = pl.BlockSpec(memory_space=pltpu.VMEM)


def cos_sin(angles):
    return np.stack([np.cos(angles), np.sin(angles)]).astype(np.float32)


def seeds():
    freqs = np.arange(1, NF + 1, dtype=np.float64) * STEP
    halves = np.arange(LAGS // 2, dtype=np.float64) + 0.5
    rows = np.zeros(32)
    rows[:16], rows[16:24], rows[24:] = np.arange(16), 16, 0.5
    lag_rows = np.full(24, 16 * STEP)
    lag_rows[:16] = freqs[:16]
    return cos_sin(rows[:, None] * freqs[None, :]), cos_sin(lag_rows[:, None] * halves[None, :])


def rotate(cosine, sine, turn_cos, turn_sin):
    return cosine * turn_cos - sine * turn_sin, sine * turn_cos + cosine * turn_sin


def fill_forward(seed, table, block, width):
    lanes = pl.ds(block * width, width)
    imag_lanes = pl.ds(NF + block * width, width)
    turn_cos, turn_sin = seed[0, 16:17, lanes], seed[1, 16:17, lanes]

    def rows(index, held):
        cosine, sine = held
        at = pl.ds(pl.multiple_of(index * 16, 16), 16)
        table[at, lanes] = cosine.astype(BF16)
        table[at, imag_lanes] = (-sine).astype(BF16)
        return rotate(cosine, sine, turn_cos, turn_sin)

    lax.fori_loop(0, NS // 32, rows, (seed[0, 0:16, lanes], seed[1, 0:16, lanes]))


def fill_lags(seed, cos_table, sin_table):
    turn_cos, turn_sin = seed[0, 16:17, :], seed[1, 16:17, :]

    def rows(index, held):
        cosine, sine = held
        at = pl.ds(pl.multiple_of(index * 16, 16), 16)
        cos_table[at, :] = cosine.astype(BF16)
        sin_table[at, :] = sine.astype(BF16)
        return rotate(cosine, sine, turn_cos, turn_sin)

    lax.fori_loop(0, NF // 16, rows, (seed[0, 0:16, :], seed[1, 0:16, :]))


def channel_group(slot):
    core, low, y = slot // 8, slot // 4 % 2, slot % 4
    return 8 * low + 2 * y + core


def unpack(count, slot_of, row_of, pieces, marks, ordered, left):
    for piece in range(count // 4):
        at = slice(row_of(piece), row_of(piece) + 4)
        for window in range(WIN):
            rows = pieces[slot_of(piece), window].astype(F32)
            ordered[window, at, :] = rows[:, : NS // 2]
            ordered[WIN + window, at, :] = rows[:, NS // 2 : NS]
            marks[window, at, :] = rows[:, NS:]
    lane = lax.broadcasted_iota(jnp.int32, (count, 128), 1)
    flags = jnp.zeros((count, 128), F32)
    for window in range(WIN):
        valid = marks[window, 0:count, :]
        flags = jnp.where(lane == window, valid, flags)
        for part in (window, WIN + window):
            rows = jnp.where(valid[:, 0:1] != 0.0, ordered[part, 0:count, :], 0.0)
            left[part * count : (part + 1) * count, :] = rows.astype(BF16)
    return flags


def transform(block, left, table, spectrum, high, low):
    width = 256
    even = lax.broadcasted_iota(jnp.int32, (1, width), 1) % 2 == 0
    at = block * width
    square = None
    total = spectrum.shape[0]
    for base in (0, NF):
        lanes = slice(base + at, base + at + width)
        both = jnp.dot(left[0 : 2 * total, :], table[:, lanes], preferred_element_type=F32)
        later = both[total:]
        value = both[:total] + jnp.where(even, -later, later)
        spectrum[:, lanes] = value
        square = value * value if square is None else square + value * value
    amplitude = jnp.sqrt(square)
    rounded = amplitude.astype(BF16)
    lanes = slice(128 + at, 128 + at + width)
    high[:, lanes] = rounded
    low[:, lanes] = (amplitude - rounded.astype(F32)).astype(BF16)


def pad(high, low):
    total = high.shape[0]
    for ref in (high, low):
        ref[:, 0:128] = jnp.zeros((total, 128), BF16)
        ref[:, 128 + NF : 256 + NF] = jnp.zeros((total, 128), BF16)


def band_table(width):
    offset = lax.broadcasted_iota(jnp.int32, (2 * width, width), 0) - lax.broadcasted_iota(
        jnp.int32, (2 * width, width), 1
    )
    return jnp.where((offset >= 128 - HALF) & (offset <= 128 + HALF), 1.0, 0.0).astype(BF16)


def whiten(block, spectrum, high, low):
    width = 256
    band = band_table(width)
    at = block * width
    around = slice(at, at + 2 * width)
    running = jnp.dot(high[:, around], band, preferred_element_type=F32)
    running += jnp.dot(low[:, around], band, preferred_element_type=F32)
    factor = 1.0 / (running * (1.0 / (2 * HALF + 1)) + EPSILON)
    lanes = slice(at, at + width), slice(NF + at, NF + at + width)
    return lanes, [spectrum[:, part] * factor for part in lanes]


def put_thirds(ref, window, rows, block, thirds):
    width = 256
    for index, third in enumerate(thirds):
        at = index * NF + block * width
        ref[window, rows, at : at + width] = third


def put_sources(block, spectrum, high, low, seed, src_ref):
    (real_lanes, imag_lanes), parts = whiten(block, spectrum, high, low)
    real, imag = (part.astype(BF16).astype(F32) for part in parts)
    turn_cos, turn_sin = seed[0, 24:25, real_lanes], seed[1, 24:25, real_lanes]
    half = real.shape[0] // WIN
    for window in range(WIN):
        rows = slice(window * half, window * half + half)
        turned_real = real[rows] * turn_cos + imag[rows] * turn_sin
        turned_imag = imag[rows] * turn_cos - real[rows] * turn_sin
        put_thirds(src_ref, window, slice(None), block, (turned_real + turned_imag, turned_imag, turned_real))


def put_receivers(block, spectrum, high, low, first, rcv_ref):
    lanes, parts = whiten(block, spectrum, high, low)
    count = spectrum.shape[0] // WIN
    rows = pl.ds(pl.multiple_of(first, count), count)
    real, imag = (part.astype(BF16).astype(F32) for part in parts)
    thirds = (real, real - imag, real + imag)
    for window in range(WIN):
        own = slice(window * count, (window + 1) * count)
        put_thirds(rcv_ref, window, rows, block, [third[own].astype(BF16) for third in thirds])


CHUNK = 8
WIDE = 256


def correlate_kernel(src_ref, rcv_ref, weights, cos_ref, sin_ref, out_ref, staged, out_sems, last_sems):
    half = rcv_ref.shape[1]
    steps = half // CHUNK
    groups = half // 16
    blocks = NF // WIDE

    back = 127 - lax.broadcasted_iota(jnp.int32, (half, 128), 1)

    def finish(even_acc, odd_acc, near, source, slot):
        even, odd = pltpu.matmul_pop(even_acc), pltpu.matmul_pop(odd_acc)
        weight = jnp.broadcast_to(near[:, source : source + 1], (half, 128))
        width = LAGS // 2
        for block in range(width // 128):
            lanes = slice(block * 128, block * 128 + 128)
            e, o = even[:, lanes], odd[:, lanes]
            staged[slot, source, :, width + block * 128 : width + block * 128 + 128] = (e - o) * weight
            flipped = jnp.take_along_axis((e + o) * weight, back, axis=1)
            staged[slot, source, :, width - block * 128 - 128 : width - block * 128] = flipped

    def cross(eight, inside, block):
        real_rows, imag_rows = [], []
        halves = []
        for part in range(WIDE // 128):
            first = block * WIDE + part * 128
            lanes = [slice(base + first, base + first + 128) for base in (0, NF, 2 * NF)]
            sent = [
                [
                    jnp.broadcast_to(src_ref[w, eight, inside : inside + 1, at], (16, 128)).astype(BF16)
                    for at in lanes
                ]
                for w in range(WIN)
            ]
            halves.append((lanes, sent))
        for g in range(groups):
            reals, imags = [], []
            for lanes, sent in halves:
                total = None
                for w in range(WIN):
                    terms = [a * rcv_ref[w, 16 * g : 16 * g + 16, at] for a, at in zip(sent[w], lanes)]
                    total = terms if total is None else [x + y for x, y in zip(total, terms)]
                real, imag = total[0] - total[1], total[0] - total[2]
                reals.append(real)
                imags.append(imag)
            real_rows.append(jnp.concatenate(reals, axis=1))
            imag_rows.append(jnp.concatenate(imags, axis=1))
        return jnp.concatenate(real_rows, axis=0), jnp.concatenate(imag_rows, axis=0)

    def near_of(chunk):
        return pltpu.roll(weights[...], lax.rem(256 - chunk * CHUNK, 128), 1)

    def put(chunk):
        slot = chunk % 2 if isinstance(chunk, int) else lax.rem(chunk, 2)
        at = pl.ds(pl.multiple_of(chunk * CHUNK, CHUNK), CHUNK)
        return pltpu.make_async_copy(staged.at[slot], out_ref.at[at], out_sems.at[slot])

    def put_one(chunk, source):
        return pltpu.make_async_copy(
            staged.at[chunk % 2, source], out_ref.at[chunk * CHUNK + source], last_sems.at[source])

    def with_accumulators(even_accs, odd_accs):
        def do_chunk(chunk, now, finishing):
            near = near_of(chunk - 1)
            slot = 1 - now

            @pl.when(chunk >= 3)
            def _():
                put(chunk - 3).wait()

            done = 0
            for block in range(blocks):
                rows = pl.ds(block * WIDE, WIDE)
                pltpu.matmul_push_rhs(cos_ref[rows, :], block % 2, 0)
                pltpu.matmul_push_rhs(sin_ref[rows, :], block % 2, 1)
                for source in range(CHUNK):
                    if finishing and (block * CHUNK + source) * CHUNK >= done * blocks * CHUNK and done < CHUNK:
                        finish(even_accs[slot][done], odd_accs[slot][done], near, done, slot)
                        done += 1
                    real, imag = cross(chunk * (CHUNK // 8) + source // 8, source % 8, block)
                    load = block % 2 if source == 0 else None
                    pltpu.matmul_acc_lhs(even_accs[now][source], real, load_staged_rhs=load)
                    pltpu.matmul_acc_lhs(odd_accs[now][source], imag, load_staged_rhs=load)

            @pl.when(chunk >= 1)
            def _():
                put(chunk - 1).start()

        def step(pair, carry):
            do_chunk(2 * pair, 0, True)
            do_chunk(2 * pair + 1, 1, True)
            return carry

        lax.fori_loop(0, steps // 2, step, 0)
        last = steps - 1
        put(last - 2).wait()
        near = near_of(last)
        for source in range(CHUNK):
            finish(even_accs[1][source], odd_accs[1][source], near, source, last % 2)
            put_one(last, source).start()
        put(last - 1).wait()
        for source in range(CHUNK):
            put_one(last, source).wait()

    pl.run_scoped(
        with_accumulators,
        [[pltpu.ACC(0)((half, LAGS // 2), F32) for _ in range(CHUNK)] for _ in range(2)],
        [[pltpu.ACC(1)((half, LAGS // 2), F32) for _ in range(CHUNK)] for _ in range(2)],
    )


def correlated(src, rcv, weights, cos_table, sin_table):
    half = rcv.shape[1]
    args = (src.reshape(WIN, half // 8, 8, 3 * NF), rcv, weights, cos_table, sin_table)
    return pl.pallas_call(
        correlate_kernel,
        out_shape=jax.ShapeDtypeStruct((half, half, LAGS), F32),
        in_specs=[VMEM] * 5,
        out_specs=pl.BlockSpec(memory_space=pl.ANY),
        scratch_shapes=[
            pltpu.VMEM((2, CHUNK, half, LAGS), F32),
            pltpu.SemaphoreType.DMA((2,)),
            pltpu.SemaphoreType.DMA((CHUNK,)),
        ],
        compiler_params=pltpu.CompilerParams(vmem_limit_bytes=8 * 2**20),
    )(*args)

MESH = pl.DeviceIdType.MESH


def spectra_kernel(traces_ref, valid_ref, seed_ref, lag_seed_ref, mask_ref,
                   src_ref, rcv_ref, weights_ref, cos_ref, sin_ref,
                   valid, seed, lag_seed, mask, flags_ref, mine, pieces, marks, table, ordered, left, spectrum, high, low_part,
                   local_sems, send_sems, recv_sems):
    s, r = lax.axis_index("src"), lax.axis_index("rcv")
    z, high_x = lax.div(s, 2), lax.rem(s, 2)
    low, y, core = lax.div(r, 8), lax.rem(lax.div(r, 2), 4), lax.rem(r, 2)

    def around(step):
        return (s, 8 * low + 2 * lax.rem(y + 4 + step, 4) + core)

    def along(step):
        return (2 * lax.rem(z + 8 + step, 8) + high_x, r)

    sibling = (s, 8 * low + 2 * y + 1 - core)
    beside = (s, 8 * (1 - low) + 2 * y + core)
    across = (2 * z + 1 - high_x, r)
    own_low = lax.rem(low + high_x + core, 2)
    mirror_x = lax.rem(high_x + low + lax.div(z, 4), 2)
    mirror = (2 * lax.rem(r, 8) + mirror_x, s)
    mirrored_from = (r, 8 * own_low + z)
    away = jnp.logical_or(mirror[0] != s, s != r)

    def src_slot(step, other):
        column = 1 - low if other else low
        return core * 8 + column * 4 + lax.rem(y + 4 + step, 4)

    def rcv_slot(step, other):
        column = 1 - own_low if other else own_low
        return 16 + column * 8 + lax.rem(z + 8 + step, 8)

    loads = [
        pltpu.make_async_copy(source, target, local_sems.at[index])
        for index, (source, target) in enumerate(
            ((traces_ref, mine.at[:, :, 0:NS]), (valid_ref, valid), (seed_ref, seed), (lag_seed_ref, lag_seed), (mask_ref, mask)))
    ]
    for load in loads:
        load.start()
    y_steps, z_steps = (1, -1, 2), (2, -2, 1, -1)
    way = 1 - 2 * core
    def diagonal(step):
        return (2 * lax.rem(z + 8 + step, 8) + 1 - high_x, r)

    peers = [diagonal(-way), diagonal(way), diagonal(-2 * way)]
    peers += [sibling, beside, across] + [around(k) for k in y_steps] + [along(k) for k in z_steps]
    barrier = pltpu.get_barrier_semaphore()
    for peer in peers:
        pl.semaphore_signal(barrier, inc=1, device_id=peer, device_id_type=MESH)

    @pl.when(away)
    def _():
        pl.semaphore_signal(barrier, inc=1, device_id=mirrored_from, device_id_type=MESH)

    def copy(slot, device, source=None):
        return pltpu.make_async_remote_copy(
            src_ref=pieces.at[slot] if source is None else source,
            dst_ref=pieces.at[slot], send_sem=send_sems.at[0],
            recv_sem=recv_sems.at[slot], device_id=device, device_id_type=MESH)

    def arrive(slot):
        block = pieces.at[slot]
        pltpu.make_async_copy(block, block, recv_sems.at[slot]).wait()

    halves = (slice(0, NS), slice(NS, NS + 128))
    home = rcv_slot(0, False)

    def place(part, source):
        away_copy = pltpu.make_async_remote_copy(
            src_ref=source, dst_ref=pieces.at[16 + r, :, :, halves[part]], send_sem=send_sems.at[1 + part],
            recv_sem=recv_sems.at[16 + r], device_id=mirror, device_id_type=MESH)

        @pl.when(away)
        def _():
            away_copy.start()

        @pl.when(jnp.logical_not(away))
        def _():
            target = pieces.at[home, :, :, halves[part]]
            pltpu.make_async_copy(source, target, recv_sems.at[home]).start()

        return away_copy

    pl.semaphore_wait(barrier, len(peers) + jnp.where(away, 1, 0))
    placed = [place(0, traces_ref)]
    loads[0].wait()
    loads[1].wait()
    for window in range(WIN):
        count = valid.shape[1]
        keep = jnp.concatenate([valid[window : window + 1, c : c + 1] for c in range(count)], axis=0)
        mine[window, :, halves[1]] = jnp.broadcast_to(jnp.where(keep != 0, 1.0, 0.0), (count, 128)).astype(BF16)
    placed.append(place(1, mine.at[:, :, halves[1]]))
    own = src_slot(0, False)
    local = pltpu.make_async_copy(mine, pieces.at[own], recv_sems.at[own])
    local.start()
    loads[2].wait()
    loads[3].wait()
    width = 256
    blocks = NF // width
    filled = iter(range(blocks))

    def fill(count):
        for _ in range(count):
            fill_forward(seed, table, next(filled), width)

    fill(2)
    for device in [beside] + [around(k) for k in y_steps] + [sibling]:
        copy(own, device, mine).start()
    fill(blocks - 2)
    fill_lags(lag_seed, cos_ref, sin_ref)
    pad(high, low_part)
    slot = rcv_slot(0, False)
    arrive(slot)
    for device in [along(k) for k in z_steps] + [across]:
        copy(slot, device).start()
    slot = src_slot(0, True)
    arrive(slot)
    for device in [around(k) for k in y_steps] + [sibling]:
        copy(slot, device).start()
    for step, onward in ((-2 * way, (2 * way, way)), (2 * way, (-way,))):
        slot = rcv_slot(step, False)
        arrive(slot)
        for further in onward:
            copy(slot, along(further)).start()
            copy(slot, diagonal(further)).start()
        copy(slot, across).start()
    slot = rcv_slot(0, True)
    arrive(slot)
    for device in (along(1), along(-1)):
        copy(slot, device).start()
    for step in y_steps:
        slot = src_slot(step, False)
        arrive(slot)
        copy(slot, sibling).start()
    for step in y_steps:
        slot = src_slot(step, True)
        arrive(slot)
        copy(slot, sibling).start()
    for index in range(8):
        arrive((1 - core) * 8 + index)
    local.wait()
    half = src_ref.shape[1]
    quarter = half // 2
    flags_ref[0:half, :] = unpack(
        half, lambda p: p, lambda p: 4 * channel_group(p), pieces, marks, ordered, left)
    for block in range(blocks):
        transform(block, left, table, spectrum, high, low_part)
    for block in range(blocks):
        put_sources(block, spectrum, high, low_part, seed, src_ref)
    views = [ref.at[0:half] for ref in (spectrum, high, low_part)]
    for batch, column in enumerate((own_low, 1 - own_low)):
        for step in range(8):
            if step not in ((0, 2, 6), (0,))[batch]:
                arrive(rcv_slot(step, batch == 1))
        base = 16 + 8 * column
        first = quarter * column
        flags_ref[pl.ds(pl.multiple_of(half + first, quarter), quarter), :] = unpack(
            quarter, lambda p: base + p, lambda p: 4 * p, pieces, marks, ordered, left)
        for block in range(blocks):
            transform(block, left, table, *views)
        for block in range(blocks):
            put_receivers(block, *views, first, rcv_ref)
    loads[4].wait()
    flip = flags_ref[0:half, :].T
    counts = sum(flags_ref[half : 2 * half, w : w + 1] * flip[w : w + 1, :] for w in range(WIN))
    scale = mask[...].astype(F32).T * (1.0 / math.sqrt(NF)) / jnp.maximum(counts, 1.0)
    weights_ref[...] = jnp.concatenate([scale, jnp.zeros((half, 128 - half), F32)], axis=1)
    block = pieces.at[pl.ds(0, 30)]
    pltpu.make_async_copy(block, block, send_sems.at[0]).wait()

    @pl.when(away)
    def _():
        for part in placed:
            part.wait_send()


def spectra(half, traces, window_valid, pair_mask):
    seed, lag_seed = seeds()
    total = WIN * half
    far = pl.BlockSpec(memory_space=pltpu.HBM)
    slot = (WIN, traces.shape[1], NS + 128)
    return pl.pallas_call(
        spectra_kernel,
        out_shape=[
            jax.ShapeDtypeStruct((WIN, half, 3 * NF), F32),
            jax.ShapeDtypeStruct((WIN, half, 3 * NF), BF16),
            jax.ShapeDtypeStruct((half, 128), F32),
            jax.ShapeDtypeStruct((NF, LAGS // 2), BF16),
            jax.ShapeDtypeStruct((NF, LAGS // 2), BF16),
        ],
        in_specs=[far] * 5,
        out_specs=[VMEM] * 5,
        scratch_shapes=[
            pltpu.VMEM(window_valid.shape, jnp.int32),
            pltpu.VMEM(seed.shape, F32),
            pltpu.VMEM(lag_seed.shape, F32),
            pltpu.VMEM(pair_mask.shape, jnp.int32),
            pltpu.VMEM((2 * half, 128), F32),
            pltpu.VMEM(slot, BF16),
            pltpu.VMEM((32,) + slot, BF16),
            pltpu.VMEM((WIN, half, 128), F32),
            pltpu.VMEM((NS // 2, NS), BF16),
            pltpu.VMEM((4, half, NS // 2), F32),
            pltpu.VMEM((2 * total, NS // 2), BF16),
            pltpu.VMEM((total, NS), F32),
            pltpu.VMEM((total, NF + 256), BF16),
            pltpu.VMEM((total, NF + 256), BF16),
            pltpu.SemaphoreType.DMA((5,)),
            pltpu.SemaphoreType.DMA((3,)),
            pltpu.SemaphoreType.DMA((32,)),
        ],
        compiler_params=pltpu.CompilerParams(
            collective_id=0, has_side_effects=True, vmem_limit_bytes=28 * 2**20),
    )(*(pltpu.with_memory_space_constraint(a, pltpu.HBM) for a in (traces, window_valid, jnp.asarray(seed), jnp.asarray(lag_seed), pair_mask)))


def shards(traces, window_valid, pair_mask):
    src, rcv, weights, cos_table, sin_table = spectra(pair_mask.shape[0], traces, window_valid, pair_mask)
    return correlated(src, rcv, weights, cos_table, sin_table)


def solution(mesh):
    in_specs = (P(None, ("src", "rcv"), None), P(None, ("src", "rcv")), P("src", "rcv"))
    mapped = jax.shard_map(
        shards, mesh=mesh, in_specs=in_specs, out_specs=P("src", "rcv", None), check_vma=False)

    def run(traces, window_valid, pair_mask):
        with jax.sharding.use_abstract_mesh(mesh.abstract_mesh):
            return mapped(traces, window_valid, pair_mask)

    return run
```

```python
import functools
import math

import jax
import jax.numpy as jnp
import numpy as np
from jax import lax
from jax.experimental import pallas as pl
from jax.experimental.pallas import tpu as pltpu
from jax.sharding import PartitionSpec as P

NS = 3072
NF = 1536
LAGS = 512
HALF = 32
WIN = 2
EPSILON = 1e-06
STEP = 2.0 * math.pi / NS
INVALID = 100.0
F32 = jnp.float32
BF16 = jnp.bfloat16
PARTS = 1
VMEM = pl.BlockSpec(memory_space=pltpu.VMEM)


def cos_sin(angles):
    return np.stack([np.cos(angles), np.sin(angles)]).astype(np.float32)


def seeds():
    freqs = np.arange(1, NF + 1, dtype=np.float64) * STEP
    halves = np.arange(LAGS // 2, dtype=np.float64) + 0.5
    rows = np.zeros(32)
    rows[:16], rows[16:24], rows[24:] = np.arange(16), 16, 0.5
    lag_rows = np.full(24, 16 * STEP)
    lag_rows[:16] = freqs[:16]
    return cos_sin(rows[:, None] * freqs[None, :]), cos_sin(lag_rows[:, None] * halves[None, :])


def rotate(cosine, sine, turn_cos, turn_sin):
    return cosine * turn_cos - sine * turn_sin, sine * turn_cos + cosine * turn_sin


def fill_forward(seed, table, block, width):
    lanes = pl.ds(block * width, width)
    imag_lanes = pl.ds(NF + block * width, width)
    turn_cos, turn_sin = seed[0, 16:17, lanes], seed[1, 16:17, lanes]

    def rows(index, held):
        cosine, sine = held
        at = pl.ds(pl.multiple_of(index * 16, 16), 16)
        table[at, lanes] = cosine.astype(BF16)
        table[at, imag_lanes] = (-sine).astype(BF16)
        return rotate(cosine, sine, turn_cos, turn_sin)

    lax.fori_loop(0, NS // 32, rows, (seed[0, 0:16, lanes], seed[1, 0:16, lanes]))


def fill_lags(seed, cos_table, sin_table):
    turn_cos, turn_sin = seed[0, 16:17, :], seed[1, 16:17, :]

    def rows(index, held):
        cosine, sine = held
        at = pl.ds(pl.multiple_of(index * 16, 16), 16)
        cos_table[at, :] = cosine.astype(BF16)
        sin_table[at, :] = sine.astype(BF16)
        return rotate(cosine, sine, turn_cos, turn_sin)

    lax.fori_loop(0, NF // 16, rows, (seed[0, 0:16, :], seed[1, 0:16, :]))


def channel_group(slot):
    core, low, y = slot // 8, slot // 4 % 2, slot % 4
    return 8 * low + 2 * y + core


def unpack(count, slot_of, row_of, pieces, ordered, left):
    for piece in range(count // 4):
        first = row_of(piece)
        width = NS // 2 // PARTS
        for index in range(PARTS):
            rows = pieces[slot_of(piece), index].astype(F32)
            lanes = slice(index * width, index * width + width)
            for part in range(4):
                ordered[part, first : first + 4, lanes] = rows[4 * part : 4 * part + 4]
    lane = lax.broadcasted_iota(jnp.int32, (count, 128), 1)
    flags = jnp.zeros((count, 128), F32)
    for window in range(WIN):
        valid = ordered[window, 0:count, 0:1] < 0.5 * INVALID
        flags = jnp.where((lane == window) & valid, 1.0, flags)
        for part in (window, WIN + window):
            rows = jnp.where(valid, ordered[part, 0:count, :], 0.0)
            left[part * count : (part + 1) * count, :] = rows.astype(BF16)
    return flags


def transform(block, left, table, spectrum, high, low):
    width = 256
    even = lax.broadcasted_iota(jnp.int32, (1, width), 1) % 2 == 0
    at = block * width
    square = None
    total = spectrum.shape[0]
    for base in (0, NF):
        lanes = slice(base + at, base + at + width)
        both = jnp.dot(left[0 : 2 * total, :], table[:, lanes], preferred_element_type=F32)
        later = both[total:]
        value = both[:total] + jnp.where(even, -later, later)
        spectrum[:, lanes] = value
        square = value * value if square is None else square + value * value
    amplitude = jnp.sqrt(square)
    rounded = amplitude.astype(BF16)
    lanes = slice(128 + at, 128 + at + width)
    high[:, lanes] = rounded
    low[:, lanes] = (amplitude - rounded.astype(F32)).astype(BF16)


def pad(high, low):
    total = high.shape[0]
    for ref in (high, low):
        ref[:, 0:128] = jnp.zeros((total, 128), BF16)
        ref[:, 128 + NF : 256 + NF] = jnp.zeros((total, 128), BF16)


def band_table(width):
    offset = lax.broadcasted_iota(jnp.int32, (2 * width, width), 0) - lax.broadcasted_iota(
        jnp.int32, (2 * width, width), 1
    )
    return jnp.where((offset >= 128 - HALF) & (offset <= 128 + HALF), 1.0, 0.0).astype(BF16)


def whiten(block, spectrum, high, low):
    width = 256
    band = band_table(width)
    at = block * width
    around = slice(at, at + 2 * width)
    running = jnp.dot(high[:, around], band, preferred_element_type=F32)
    running += jnp.dot(low[:, around], band, preferred_element_type=F32)
    factor = 1.0 / (running * (1.0 / (2 * HALF + 1)) + EPSILON)
    lanes = slice(at, at + width), slice(NF + at, NF + at + width)
    return lanes, [spectrum[:, part] * factor for part in lanes]


def put_thirds(ref, window, rows, block, thirds):
    width = 256
    for index, third in enumerate(thirds):
        at = index * NF + block * width
        ref[window, rows, at : at + width] = third


def put_sources(block, spectrum, high, low, seed, src_ref):
    (real_lanes, imag_lanes), parts = whiten(block, spectrum, high, low)
    real, imag = (part.astype(BF16).astype(F32) for part in parts)
    turn_cos, turn_sin = seed[0, 24:25, real_lanes], seed[1, 24:25, real_lanes]
    half = real.shape[0] // WIN
    for window in range(WIN):
        rows = slice(window * half, window * half + half)
        turned_real = real[rows] * turn_cos + imag[rows] * turn_sin
        turned_imag = imag[rows] * turn_cos - real[rows] * turn_sin
        put_thirds(src_ref, window, slice(None), block, (turned_real + turned_imag, turned_imag, turned_real))


def put_receivers(block, spectrum, high, low, first, rcv_ref):
    lanes, parts = whiten(block, spectrum, high, low)
    count = spectrum.shape[0] // WIN
    rows = pl.ds(pl.multiple_of(first, count), count)
    real, imag = (part.astype(BF16) for part in parts)
    thirds = (real, real - imag, real + imag)
    for window in range(WIN):
        own = slice(window * count, (window + 1) * count)
        put_thirds(rcv_ref, window, rows, block, [third[own] for third in thirds])


CHUNK = 8
WIDE = 256


def correlate_kernel(src_ref, rcv_ref, weights, cos_ref, sin_ref, out_ref, staged, out_sems, last_sems):
    half = rcv_ref.shape[1]
    steps = half // CHUNK
    groups = half // 16
    blocks = NF // WIDE

    back = 127 - lax.broadcasted_iota(jnp.int32, (half, 128), 1)

    def finish(even_acc, odd_acc, near, source, slot):
        even, odd = pltpu.matmul_pop(even_acc), pltpu.matmul_pop(odd_acc)
        weight = jnp.broadcast_to(near[:, source : source + 1], (half, 128))
        width = LAGS // 2
        for block in range(width // 128):
            lanes = slice(block * 128, block * 128 + 128)
            e, o = even[:, lanes], odd[:, lanes]
            staged[slot, source, :, width + block * 128 : width + block * 128 + 128] = (e - o) * weight
            flipped = jnp.take_along_axis((e + o) * weight, back, axis=1)
            staged[slot, source, :, width - block * 128 - 128 : width - block * 128] = flipped

    def cross(eight, inside, block):
        real_rows, imag_rows = [], []
        halves = []
        for part in range(WIDE // 128):
            first = block * WIDE + part * 128
            lanes = [slice(base + first, base + first + 128) for base in (0, NF, 2 * NF)]
            sent = [
                [
                    jnp.broadcast_to(src_ref[w, eight, inside : inside + 1, at], (16, 128)).astype(BF16)
                    for at in lanes
                ]
                for w in range(WIN)
            ]
            halves.append((lanes, sent))
        for g in range(groups):
            reals, imags = [], []
            for lanes, sent in halves:
                total = None
                for w in range(WIN):
                    terms = [a * rcv_ref[w, 16 * g : 16 * g + 16, at] for a, at in zip(sent[w], lanes)]
                    total = terms if total is None else [x + y for x, y in zip(total, terms)]
                real, imag = total[0] - total[1], total[0] - total[2]
                reals.append(real)
                imags.append(imag)
            real_rows.append(jnp.concatenate(reals, axis=1))
            imag_rows.append(jnp.concatenate(imags, axis=1))
        return jnp.concatenate(real_rows, axis=0), jnp.concatenate(imag_rows, axis=0)

    def near_of(chunk):
        return pltpu.roll(weights[...], lax.rem(256 - chunk * CHUNK, 128), 1)

    def put(chunk):
        slot = chunk % 2 if isinstance(chunk, int) else lax.rem(chunk, 2)
        at = pl.ds(pl.multiple_of(chunk * CHUNK, CHUNK), CHUNK)
        return pltpu.make_async_copy(staged.at[slot], out_ref.at[at], out_sems.at[slot])

    def put_one(chunk, source):
        return pltpu.make_async_copy(
            staged.at[chunk % 2, source], out_ref.at[chunk * CHUNK + source], last_sems.at[source])

    def with_accumulators(even_accs, odd_accs):
        def do_chunk(chunk, now, finishing):
            near = near_of(chunk - 1)
            slot = 1 - now

            @pl.when(chunk >= 3)
            def _():
                put(chunk - 3).wait()

            done = 0
            for block in range(blocks):
                rows = pl.ds(block * WIDE, WIDE)
                pltpu.matmul_push_rhs(cos_ref[rows, :], block % 2, 0)
                pltpu.matmul_push_rhs(sin_ref[rows, :], block % 2, 1)
                for source in range(CHUNK):
                    if finishing and (block * CHUNK + source) * CHUNK >= done * blocks * CHUNK and done < CHUNK:
                        finish(even_accs[slot][done], odd_accs[slot][done], near, done, slot)
                        done += 1
                    real, imag = cross(chunk * (CHUNK // 8) + source // 8, source % 8, block)
                    load = block % 2 if source == 0 else None
                    pltpu.matmul_acc_lhs(even_accs[now][source], real, load_staged_rhs=load)
                    pltpu.matmul_acc_lhs(odd_accs[now][source], imag, load_staged_rhs=load)

            @pl.when(chunk >= 1)
            def _():
                put(chunk - 1).start()

        def step(pair, carry):
            do_chunk(2 * pair, 0, True)
            do_chunk(2 * pair + 1, 1, True)
            return carry

        lax.fori_loop(0, steps // 2, step, 0)
        last = steps - 1
        put(last - 2).wait()
        near = near_of(last)
        for source in range(CHUNK):
            finish(even_accs[1][source], odd_accs[1][source], near, source, last % 2)
            put_one(last, source).start()
        put(last - 1).wait()
        for source in range(CHUNK):
            put_one(last, source).wait()

    pl.run_scoped(
        with_accumulators,
        [[pltpu.ACC(0)((half, LAGS // 2), F32) for _ in range(CHUNK)] for _ in range(2)],
        [[pltpu.ACC(1)((half, LAGS // 2), F32) for _ in range(CHUNK)] for _ in range(2)],
    )


def correlated(src, rcv, weights, cos_table, sin_table):
    half = rcv.shape[1]
    args = (src.reshape(WIN, half // 8, 8, 3 * NF), rcv, weights, cos_table, sin_table)
    return pl.pallas_call(
        correlate_kernel,
        out_shape=jax.ShapeDtypeStruct((half, half, LAGS), F32),
        in_specs=[VMEM] * 5,
        out_specs=pl.BlockSpec(memory_space=pl.ANY),
        scratch_shapes=[
            pltpu.VMEM((2, CHUNK, half, LAGS), F32),
            pltpu.SemaphoreType.DMA((2,)),
            pltpu.SemaphoreType.DMA((CHUNK,)),
        ],
        compiler_params=pltpu.CompilerParams(vmem_limit_bytes=8 * 2**20),
    )(*args)

MESH = pl.DeviceIdType.MESH


def spectra_kernel(traces_ref, valid_ref, seed_ref, lag_seed_ref, mask_ref,
                   src_ref, rcv_ref, weights_ref, cos_ref, sin_ref,
                   traces, valid, seed, lag_seed, mask, flags_ref, mine, pieces, table, ordered, left, spectrum, high, low_part,
                   local_sems, send_sems, recv_sems):
    s, r = lax.axis_index("src"), lax.axis_index("rcv")
    z, high_x = lax.div(s, 2), lax.rem(s, 2)
    low, y, core = lax.div(r, 8), lax.rem(lax.div(r, 2), 4), lax.rem(r, 2)

    def around(step):
        return (s, 8 * low + 2 * lax.rem(y + 4 + step, 4) + core)

    def along(step):
        return (2 * lax.rem(z + 8 + step, 8) + high_x, r)

    sibling = (s, 8 * low + 2 * y + 1 - core)
    beside = (s, 8 * (1 - low) + 2 * y + core)
    across = (2 * z + 1 - high_x, r)
    own_low = lax.rem(low + high_x + core, 2)
    mirror_x = lax.rem(high_x + low + lax.div(z, 4), 2)
    mirror = (2 * lax.rem(r, 8) + mirror_x, s)
    mirrored_from = (r, 8 * own_low + z)
    away = jnp.logical_or(mirror[0] != s, s != r)

    def src_slot(step, other):
        column = 1 - low if other else low
        return core * 8 + column * 4 + lax.rem(y + 4 + step, 4)

    def rcv_slot(step, other):
        column = 1 - own_low if other else own_low
        return 16 + column * 8 + lax.rem(z + 8 + step, 8)

    loads = [
        pltpu.make_async_copy(source, target, local_sems.at[index])
        for index, (source, target) in enumerate(
            ((traces_ref, traces), (valid_ref, valid), (seed_ref, seed), (lag_seed_ref, lag_seed), (mask_ref, mask)))
    ]
    for load in loads:
        load.start()
    y_steps, z_steps = (1, -1, 2), (2, -2, 1, -1)
    way = 1 - 2 * core
    def diagonal(step):
        return (2 * lax.rem(z + 8 + step, 8) + 1 - high_x, r)

    peers = [diagonal(-way), diagonal(way), diagonal(-2 * way)]
    peers += [sibling, beside, across] + [around(k) for k in y_steps] + [along(k) for k in z_steps]
    barrier = pltpu.get_barrier_semaphore()
    for peer in peers:
        pl.semaphore_signal(barrier, inc=1, device_id=peer, device_id_type=MESH)

    @pl.when(away)
    def _():
        pl.semaphore_signal(barrier, inc=1, device_id=mirrored_from, device_id_type=MESH)

    def copy(slot, device, source=None, part=None, sem=0):
        target = pieces.at[slot] if part is None else pieces.at[slot, part]
        return pltpu.make_async_remote_copy(
            src_ref=target if source is None else source,
            dst_ref=target, send_sem=send_sems.at[sem],
            recv_sem=recv_sems.at[slot, part or 0], device_id=device, device_id_type=MESH)

    def arrive(slot, part=None):
        block = pieces.at[slot] if part is None else pieces.at[slot, part]
        pltpu.make_async_copy(block, block, recv_sems.at[slot, part or 0]).wait()

    loads[0].wait()
    loads[1].wait()
    samples = NS // 2
    parts = []
    for window in range(WIN):
        rows = traces[window].astype(F32)
        keep = jnp.concatenate([valid[window : window + 1, c : c + 1] for c in range(rows.shape[0])], axis=0)
        parts.append(jnp.where(keep != 0, rows, INVALID))
    width = samples // PARTS
    for index in range(PARTS):
        starts = [first + index * width for first in (0, samples)]
        mine[index] = jnp.concatenate(
            [part[:, at : at + width] for at in starts for part in parts], axis=0).astype(BF16)

    own = src_slot(0, False)
    local = pltpu.make_async_copy(mine, pieces.at[own], recv_sems.at[own, 0])
    local.start()
    pl.semaphore_wait(barrier, len(peers) + jnp.where(away, 1, 0))
    mirrored = [
        copy(16 + r, mirror, mine.at[part], part, 1 + part)
        for part in range(PARTS)
    ]

    @pl.when(away)
    def _():
        for part in range(PARTS):
            mirrored[part].start()

    @pl.when(jnp.logical_not(away))
    def _():
        slot = rcv_slot(0, False)
        for part in range(PARTS):
            pltpu.make_async_copy(mine.at[part], pieces.at[slot, part], recv_sems.at[slot, part]).start()

    loads[2].wait()
    loads[3].wait()
    width = 256
    blocks = NF // width
    filled = iter(range(blocks))

    def fill(count):
        for _ in range(count):
            fill_forward(seed, table, next(filled), width)

    fill(2)
    for device in [beside] + [around(k) for k in y_steps] + [sibling]:
        copy(own, device, mine).start()
    fill(blocks - 2)
    fill_lags(lag_seed, cos_ref, sin_ref)
    pad(high, low_part)
    slot = rcv_slot(0, False)
    for part in range(PARTS):
        arrive(slot, part)
        for device in [along(k) for k in z_steps] + [across]:
            copy(slot, device, None, part).start()
    slot = src_slot(0, True)
    arrive(slot)
    for device in [around(k) for k in y_steps] + [sibling]:
        copy(slot, device).start()
    for part in range(PARTS):
        for step, onward in ((-2 * way, (2 * way, way)), (2 * way, (-way,))):
            slot = rcv_slot(step, False)
            arrive(slot, part)
            for further in onward:
                copy(slot, along(further), None, part).start()
                copy(slot, diagonal(further), None, part).start()
            copy(slot, across, None, part).start()
    slot = rcv_slot(0, True)
    for part in range(PARTS):
        arrive(slot, part)
        for device in (along(1), along(-1)):
            copy(slot, device, None, part).start()
    for step in y_steps:
        slot = src_slot(step, False)
        arrive(slot)
        copy(slot, sibling).start()
    for step in y_steps:
        slot = src_slot(step, True)
        arrive(slot)
        copy(slot, sibling).start()
    for index in range(8):
        arrive((1 - core) * 8 + index)
    local.wait()
    half = src_ref.shape[1]
    quarter = half // 2
    flags_ref[0:half, :] = unpack(
        half, lambda p: p, lambda p: 4 * channel_group(p), pieces, ordered, left)
    for block in range(blocks):
        transform(block, left, table, spectrum, high, low_part)
    for block in range(blocks):
        put_sources(block, spectrum, high, low_part, seed, src_ref)
    loads[4].wait()
    views = [ref.at[0:half] for ref in (spectrum, high, low_part)]
    for batch, column in enumerate((own_low, 1 - own_low)):
        for step in range(8):
            if step not in ((0, 2, 6), (0,))[batch]:
                arrive(rcv_slot(step, batch == 1), 0)
        base = 16 + 8 * column
        first = quarter * column
        flags_ref[pl.ds(pl.multiple_of(half + first, quarter), quarter), :] = unpack(
            quarter, lambda p: base + p, lambda p: 4 * p, pieces, ordered, left)
        if batch == 1:
            flip = flags_ref[0:half, :].T
            counts = sum(flags_ref[half : 2 * half, w : w + 1] * flip[w : w + 1, :] for w in range(WIN))
            scale = mask[...].astype(F32).T * (1.0 / math.sqrt(NF)) / jnp.maximum(counts, 1.0)
            weights_ref[...] = jnp.concatenate([scale, jnp.zeros((half, 128 - half), F32)], axis=1)
        for block in range(blocks):
            transform(block, left, table, *views)
        for block in range(blocks):
            put_receivers(block, *views, first, rcv_ref)
    block = pieces.at[pl.ds(0, 30)]
    pltpu.make_async_copy(block, block, send_sems.at[0]).wait()

    @pl.when(away)
    def _():
        for part in range(PARTS):
            mirrored[part].wait_send()


def spectra(half, traces, window_valid, pair_mask):
    seed, lag_seed = seeds()
    total = WIN * half
    far = pl.BlockSpec(memory_space=pltpu.HBM)
    rows = 2 * WIN * traces.shape[1]
    return pl.pallas_call(
        spectra_kernel,
        out_shape=[
            jax.ShapeDtypeStruct((WIN, half, 3 * NF), F32),
            jax.ShapeDtypeStruct((WIN, half, 3 * NF), BF16),
            jax.ShapeDtypeStruct((half, 128), F32),
            jax.ShapeDtypeStruct((NF, LAGS // 2), BF16),
            jax.ShapeDtypeStruct((NF, LAGS // 2), BF16),
        ],
        in_specs=[far] * 5,
        out_specs=[VMEM] * 5,
        scratch_shapes=[
            pltpu.VMEM(traces.shape, BF16),
            pltpu.VMEM(window_valid.shape, jnp.int32),
            pltpu.VMEM(seed.shape, F32),
            pltpu.VMEM(lag_seed.shape, F32),
            pltpu.VMEM(pair_mask.shape, jnp.int32),
            pltpu.VMEM((2 * half, 128), F32),
            pltpu.VMEM((PARTS, rows, NS // 2 // PARTS), BF16),
            pltpu.VMEM((32, PARTS, rows, NS // 2 // PARTS), BF16),
            pltpu.VMEM((NS // 2, NS), BF16),
            pltpu.VMEM((4, half, NS // 2), F32),
            pltpu.VMEM((2 * total, NS // 2), BF16),
            pltpu.VMEM((total, NS), F32),
            pltpu.VMEM((total, NF + 256), BF16),
            pltpu.VMEM((total, NF + 256), BF16),
            pltpu.SemaphoreType.DMA((5,)),
            pltpu.SemaphoreType.DMA((1 + PARTS,)),
            pltpu.SemaphoreType.DMA((32, PARTS)),
        ],
        compiler_params=pltpu.CompilerParams(
            collective_id=0, has_side_effects=True, vmem_limit_bytes=28 * 2**20),
    )(*(pltpu.with_memory_space_constraint(a, pltpu.HBM) for a in (traces, window_valid, jnp.asarray(seed), jnp.asarray(lag_seed), pair_mask)))


def shards(traces, window_valid, pair_mask):
    src, rcv, weights, cos_table, sin_table = spectra(pair_mask.shape[0], traces, window_valid, pair_mask)
    return correlated(src, rcv, weights, cos_table, sin_table)


def solution(mesh):
    in_specs = (P(None, ("src", "rcv"), None), P(None, ("src", "rcv")), P("src", "rcv"))
    mapped = jax.shard_map(
        shards, mesh=mesh, in_specs=in_specs, out_specs=P("src", "rcv", None), check_vma=False)

    def run(traces, window_valid, pair_mask):
        with jax.sharding.use_abstract_mesh(mesh.abstract_mesh):
            return mapped(traces, window_valid, pair_mask)

    return run
```

```python
import functools
import math

import jax
import jax.numpy as jnp
import numpy as np
from jax import lax
from jax.experimental import pallas as pl
from jax.experimental.pallas import tpu as pltpu
from jax.sharding import PartitionSpec as P

NS = 3072
NF = 1536
LAGS = 512
HALF = 32
WIN = 2
EPSILON = 1e-06
STEP = 2.0 * math.pi / NS
INVALID = 100.0
F32 = jnp.float32
BF16 = jnp.bfloat16
PARTS = 1
VMEM = pl.BlockSpec(memory_space=pltpu.VMEM)


def cos_sin(angles):
    return np.stack([np.cos(angles), np.sin(angles)]).astype(np.float32)


def seeds():
    freqs = np.arange(1, NF + 1, dtype=np.float64) * STEP
    halves = np.arange(LAGS // 2, dtype=np.float64) + 0.5
    rows = np.zeros(32)
    rows[:16], rows[16:24], rows[24:] = np.arange(16), 16, 0.5
    lag_rows = np.full(24, 16 * STEP)
    lag_rows[:16] = freqs[:16]
    return cos_sin(rows[:, None] * freqs[None, :]), cos_sin(lag_rows[:, None] * halves[None, :])


def rotate(cosine, sine, turn_cos, turn_sin):
    return cosine * turn_cos - sine * turn_sin, sine * turn_cos + cosine * turn_sin


def fill_forward(seed, table, block, width):
    lanes = pl.ds(block * width, width)
    imag_lanes = pl.ds(NF + block * width, width)
    turn_cos, turn_sin = seed[0, 16:17, lanes], seed[1, 16:17, lanes]

    def rows(index, held):
        cosine, sine = held
        at = pl.ds(pl.multiple_of(index * 16, 16), 16)
        table[at, lanes] = cosine.astype(BF16)
        table[at, imag_lanes] = (-sine).astype(BF16)
        return rotate(cosine, sine, turn_cos, turn_sin)

    lax.fori_loop(0, NS // 32, rows, (seed[0, 0:16, lanes], seed[1, 0:16, lanes]))


def fill_lags(seed, cos_table, sin_table):
    turn_cos, turn_sin = seed[0, 16:17, :], seed[1, 16:17, :]

    def rows(index, held):
        cosine, sine = held
        at = pl.ds(pl.multiple_of(index * 16, 16), 16)
        cos_table[at, :] = cosine.astype(BF16)
        sin_table[at, :] = sine.astype(BF16)
        return rotate(cosine, sine, turn_cos, turn_sin)

    lax.fori_loop(0, NF // 16, rows, (seed[0, 0:16, :], seed[1, 0:16, :]))


def channel_group(slot):
    core, low, y = slot // 8, slot // 4 % 2, slot % 4
    return 8 * low + 2 * y + core


def unpack(count, slot_of, row_of, pieces, ordered, left):
    for piece in range(count // 4):
        first = row_of(piece)
        width = NS // 2 // PARTS
        for index in range(PARTS):
            rows = pieces[slot_of(piece), index].astype(F32)
            lanes = slice(index * width, index * width + width)
            for part in range(4):
                ordered[part, first : first + 4, lanes] = rows[4 * part : 4 * part + 4]
    lane = lax.broadcasted_iota(jnp.int32, (count, 128), 1)
    flags = jnp.zeros((count, 128), F32)
    for window in range(WIN):
        valid = ordered[window, 0:count, 0:1] < 0.5 * INVALID
        flags = jnp.where((lane == window) & valid, 1.0, flags)
        for part in (window, WIN + window):
            rows = jnp.where(valid, ordered[part, 0:count, :], 0.0)
            left[part * count : (part + 1) * count, :] = rows.astype(BF16)
    return flags


def transform(block, left, table, spectrum, high, low):
    width = 256
    even = lax.broadcasted_iota(jnp.int32, (1, width), 1) % 2 == 0
    at = block * width
    square = None
    total = spectrum.shape[0]
    for base in (0, NF):
        lanes = slice(base + at, base + at + width)
        both = jnp.dot(left[0 : 2 * total, :], table[:, lanes], preferred_element_type=F32)
        later = both[total:]
        value = both[:total] + jnp.where(even, -later, later)
        spectrum[:, lanes] = value
        square = value * value if square is None else square + value * value
    amplitude = jnp.sqrt(square)
    rounded = amplitude.astype(BF16)
    lanes = slice(128 + at, 128 + at + width)
    high[:, lanes] = rounded
    low[:, lanes] = (amplitude - rounded.astype(F32)).astype(BF16)


def pad(high, low):
    total = high.shape[0]
    for ref in (high, low):
        ref[:, 0:128] = jnp.zeros((total, 128), BF16)
        ref[:, 128 + NF : 256 + NF] = jnp.zeros((total, 128), BF16)


def band_table(width):
    offset = lax.broadcasted_iota(jnp.int32, (2 * width, width), 0) - lax.broadcasted_iota(
        jnp.int32, (2 * width, width), 1
    )
    return jnp.where((offset >= 128 - HALF) & (offset <= 128 + HALF), 1.0, 0.0).astype(BF16)


def whiten(block, spectrum, high, low):
    width = 256
    band = band_table(width)
    at = block * width
    around = slice(at, at + 2 * width)
    running = jnp.dot(high[:, around], band, preferred_element_type=F32)
    running += jnp.dot(low[:, around], band, preferred_element_type=F32)
    factor = 1.0 / (running * (1.0 / (2 * HALF + 1)) + EPSILON)
    lanes = slice(at, at + width), slice(NF + at, NF + at + width)
    return lanes, [spectrum[:, part] * factor for part in lanes]


def put_thirds(ref, window, rows, block, thirds):
    width = 256
    for index, third in enumerate(thirds):
        at = index * NF + block * width
        ref[window, rows, at : at + width] = third


def put_sources(block, spectrum, high, low, seed, src_ref):
    (real_lanes, imag_lanes), parts = whiten(block, spectrum, high, low)
    real, imag = (part.astype(BF16).astype(F32) for part in parts)
    turn_cos, turn_sin = seed[0, 24:25, real_lanes], seed[1, 24:25, real_lanes]
    half = real.shape[0] // WIN
    for window in range(WIN):
        rows = slice(window * half, window * half + half)
        turned_real = real[rows] * turn_cos + imag[rows] * turn_sin
        turned_imag = imag[rows] * turn_cos - real[rows] * turn_sin
        put_thirds(src_ref, window, slice(None), block, (turned_real + turned_imag, turned_imag, turned_real))


def put_receivers(block, spectrum, high, low, first, rcv_ref):
    lanes, parts = whiten(block, spectrum, high, low)
    count = spectrum.shape[0] // WIN
    rows = pl.ds(pl.multiple_of(first, count), count)
    real, imag = (part.astype(BF16) for part in parts)
    thirds = (real, real - imag, real + imag)
    for window in range(WIN):
        own = slice(window * count, (window + 1) * count)
        put_thirds(rcv_ref, window, rows, block, [third[own] for third in thirds])


CHUNK = 8
WIDE = 256


def correlate_kernel(src_ref, rcv_ref, weights, cos_ref, sin_ref, out_ref, staged, out_sems, last_sems):
    half = rcv_ref.shape[1]
    steps = half // CHUNK
    groups = half // 16
    blocks = NF // WIDE

    back = 127 - lax.broadcasted_iota(jnp.int32, (half, 128), 1)

    def finish(even_acc, odd_acc, near, source, slot):
        even, odd = pltpu.matmul_pop(even_acc), pltpu.matmul_pop(odd_acc)
        weight = jnp.broadcast_to(near[:, source : source + 1], (half, 128))
        width = LAGS // 2
        for block in range(width // 128):
            lanes = slice(block * 128, block * 128 + 128)
            e, o = even[:, lanes], odd[:, lanes]
            staged[slot, source, :, width + block * 128 : width + block * 128 + 128] = (e - o) * weight
            flipped = jnp.take_along_axis((e + o) * weight, back, axis=1)
            staged[slot, source, :, width - block * 128 - 128 : width - block * 128] = flipped

    def cross(eight, inside, block):
        real_rows, imag_rows = [], []
        halves = []
        for part in range(WIDE // 128):
            first = block * WIDE + part * 128
            lanes = [slice(base + first, base + first + 128) for base in (0, NF, 2 * NF)]
            sent = [
                [
                    jnp.broadcast_to(src_ref[w, eight, inside : inside + 1, at], (16, 128)).astype(BF16)
                    for at in lanes
                ]
                for w in range(WIN)
            ]
            halves.append((lanes, sent))
        for g in range(groups):
            reals, imags = [], []
            for lanes, sent in halves:
                total = None
                for w in range(WIN):
                    terms = [a * rcv_ref[w, 16 * g : 16 * g + 16, at] for a, at in zip(sent[w], lanes)]
                    total = terms if total is None else [x + y for x, y in zip(total, terms)]
                real, imag = total[0] - total[1], total[0] - total[2]
                reals.append(real)
                imags.append(imag)
            real_rows.append(jnp.concatenate(reals, axis=1))
            imag_rows.append(jnp.concatenate(imags, axis=1))
        return jnp.concatenate(real_rows, axis=0), jnp.concatenate(imag_rows, axis=0)

    def near_of(chunk):
        return pltpu.roll(weights[...], lax.rem(256 - chunk * CHUNK, 128), 1)

    def put(chunk):
        slot = chunk % 2 if isinstance(chunk, int) else lax.rem(chunk, 2)
        at = pl.ds(pl.multiple_of(chunk * CHUNK, CHUNK), CHUNK)
        return pltpu.make_async_copy(staged.at[slot], out_ref.at[at], out_sems.at[slot])

    def put_one(chunk, source):
        return pltpu.make_async_copy(
            staged.at[chunk % 2, source], out_ref.at[chunk * CHUNK + source], last_sems.at[source])

    def with_accumulators(even_accs, odd_accs):
        def do_chunk(chunk, now, finishing):
            near = near_of(chunk - 1)
            slot = 1 - now

            @pl.when(chunk >= 3)
            def _():
                put(chunk - 3).wait()

            done = 0
            for block in range(blocks):
                rows = pl.ds(block * WIDE, WIDE)
                pltpu.matmul_push_rhs(cos_ref[rows, :], block % 2, 0)
                pltpu.matmul_push_rhs(sin_ref[rows, :], block % 2, 1)
                for source in range(CHUNK):
                    if finishing and (block * CHUNK + source) * CHUNK >= done * blocks * CHUNK and done < CHUNK:
                        finish(even_accs[slot][done], odd_accs[slot][done], near, done, slot)
                        done += 1
                    real, imag = cross(chunk * (CHUNK // 8) + source // 8, source % 8, block)
                    load = block % 2 if source == 0 else None
                    pltpu.matmul_acc_lhs(even_accs[now][source], real, load_staged_rhs=load)
                    pltpu.matmul_acc_lhs(odd_accs[now][source], imag, load_staged_rhs=load)

            @pl.when(chunk >= 1)
            def _():
                put(chunk - 1).start()

        def step(pair, carry):
            do_chunk(2 * pair, 0, True)
            do_chunk(2 * pair + 1, 1, True)
            return carry

        lax.fori_loop(0, steps // 2, step, 0)
        last = steps - 1
        put(last - 2).wait()
        near = near_of(last)
        for source in range(CHUNK):
            finish(even_accs[1][source], odd_accs[1][source], near, source, last % 2)
            put_one(last, source).start()
        put(last - 1).wait()
        for source in range(CHUNK):
            put_one(last, source).wait()

    pl.run_scoped(
        with_accumulators,
        [[pltpu.ACC(0)((half, LAGS // 2), F32) for _ in range(CHUNK)] for _ in range(2)],
        [[pltpu.ACC(1)((half, LAGS // 2), F32) for _ in range(CHUNK)] for _ in range(2)],
    )


def correlated(src, rcv, weights, cos_table, sin_table):
    half = rcv.shape[1]
    args = (src.reshape(WIN, half // 8, 8, 3 * NF), rcv, weights, cos_table, sin_table)
    return pl.pallas_call(
        correlate_kernel,
        out_shape=jax.ShapeDtypeStruct((half, half, LAGS), F32),
        in_specs=[VMEM] * 5,
        out_specs=pl.BlockSpec(memory_space=pl.ANY),
        scratch_shapes=[
            pltpu.VMEM((2, CHUNK, half, LAGS), F32),
            pltpu.SemaphoreType.DMA((2,)),
            pltpu.SemaphoreType.DMA((CHUNK,)),
        ],
        compiler_params=pltpu.CompilerParams(vmem_limit_bytes=8 * 2**20),
    )(*args)

MESH = pl.DeviceIdType.MESH


def spectra_kernel(traces_ref, valid_ref, seed_ref, lag_seed_ref, mask_ref,
                   src_ref, rcv_ref, weights_ref, cos_ref, sin_ref,
                   traces, valid, seed, lag_seed, mask, flags_ref, mine, pieces, table, ordered, left, spectrum, high, low_part,
                   local_sems, send_sems, recv_sems):
    s, r = lax.axis_index("src"), lax.axis_index("rcv")
    z, high_x = lax.div(s, 2), lax.rem(s, 2)
    low, y, core = lax.div(r, 8), lax.rem(lax.div(r, 2), 4), lax.rem(r, 2)

    def around(step):
        return (s, 8 * low + 2 * lax.rem(y + 4 + step, 4) + core)

    def along(step):
        return (2 * lax.rem(z + 8 + step, 8) + high_x, r)

    sibling = (s, 8 * low + 2 * y + 1 - core)
    beside = (s, 8 * (1 - low) + 2 * y + core)
    across = (2 * z + 1 - high_x, r)
    own_low = lax.rem(low + high_x + core, 2)
    mirror_x = lax.rem(high_x + low + lax.div(z, 4), 2)
    mirror = (2 * lax.rem(r, 8) + mirror_x, s)
    mirrored_from = (r, 8 * own_low + z)
    away = jnp.logical_or(mirror[0] != s, s != r)

    def src_slot(step, other):
        column = 1 - low if other else low
        return core * 8 + column * 4 + lax.rem(y + 4 + step, 4)

    def rcv_slot(step, other):
        column = 1 - own_low if other else own_low
        return 16 + column * 8 + lax.rem(z + 8 + step, 8)

    loads = [
        pltpu.make_async_copy(source, target, local_sems.at[index])
        for index, (source, target) in enumerate(
            ((traces_ref, traces), (valid_ref, valid), (seed_ref, seed), (lag_seed_ref, lag_seed), (mask_ref, mask)))
    ]
    for load in loads:
        load.start()
    y_steps, z_steps = (1, -1, 2), (2, -2, 1, -1)
    way = 1 - 2 * core
    def diagonal(step):
        return (2 * lax.rem(z + 8 + step, 8) + 1 - high_x, r)

    peers = [diagonal(-way), diagonal(way), diagonal(-2 * way)]
    peers += [sibling, beside, across] + [around(k) for k in y_steps] + [along(k) for k in z_steps]
    barrier = pltpu.get_barrier_semaphore()
    for peer in peers:
        pl.semaphore_signal(barrier, inc=1, device_id=peer, device_id_type=MESH)

    @pl.when(away)
    def _():
        pl.semaphore_signal(barrier, inc=1, device_id=mirrored_from, device_id_type=MESH)

    def copy(slot, device, source=None, part=None, sem=0):
        target = pieces.at[slot] if part is None else pieces.at[slot, part]
        return pltpu.make_async_remote_copy(
            src_ref=target if source is None else source,
            dst_ref=target, send_sem=send_sems.at[sem],
            recv_sem=recv_sems.at[slot, part or 0], device_id=device, device_id_type=MESH)

    def arrive(slot, part=None):
        block = pieces.at[slot] if part is None else pieces.at[slot, part]
        pltpu.make_async_copy(block, block, recv_sems.at[slot, part or 0]).wait()

    loads[0].wait()
    loads[1].wait()
    samples = NS // 2
    parts = []
    for window in range(WIN):
        rows = traces[window].astype(F32)
        keep = jnp.concatenate([valid[window : window + 1, c : c + 1] for c in range(rows.shape[0])], axis=0)
        parts.append(jnp.where(keep != 0, rows, INVALID))
    width = samples // PARTS
    for index in range(PARTS):
        starts = [first + index * width for first in (0, samples)]
        mine[index] = jnp.concatenate(
            [part[:, at : at + width] for at in starts for part in parts], axis=0).astype(BF16)

    own = src_slot(0, False)
    local = pltpu.make_async_copy(mine, pieces.at[own], recv_sems.at[own, 0])
    local.start()
    pl.semaphore_wait(barrier, len(peers) + jnp.where(away, 1, 0))
    mirrored = [
        copy(16 + r, mirror, mine.at[part], part, 1 + part)
        for part in range(PARTS)
    ]

    @pl.when(away)
    def _():
        for part in range(PARTS):
            mirrored[part].start()

    @pl.when(jnp.logical_not(away))
    def _():
        slot = rcv_slot(0, False)
        for part in range(PARTS):
            pltpu.make_async_copy(mine.at[part], pieces.at[slot, part], recv_sems.at[slot, part]).start()

    loads[2].wait()
    loads[3].wait()
    width = 256
    blocks = NF // width
    filled = iter(range(blocks))

    def fill(count):
        for _ in range(count):
            fill_forward(seed, table, next(filled), width)

    for device in [beside] + [around(k) for k in y_steps] + [sibling]:
        copy(own, device, mine).start()
    fill(3)
    slot = src_slot(0, True)
    arrive(slot)
    for device in [around(k) for k in y_steps] + [sibling]:
        copy(slot, device).start()
    fill(blocks - 3)
    fill_lags(lag_seed, cos_ref, sin_ref)
    pad(high, low_part)
    for step in y_steps:
        slot = src_slot(step, False)
        arrive(slot)
        copy(slot, sibling).start()
    slot = rcv_slot(0, False)
    for part in range(PARTS):
        arrive(slot, part)
        for device in [along(k) for k in z_steps] + [across]:
            copy(slot, device, None, part).start()
    for step in y_steps:
        slot = src_slot(step, True)
        arrive(slot)
        copy(slot, sibling).start()
    for part in range(PARTS):
        for step, onward in ((-2 * way, (2 * way, way)), (2 * way, (-way,))):
            slot = rcv_slot(step, False)
            arrive(slot, part)
            for further in onward:
                copy(slot, along(further), None, part).start()
                copy(slot, diagonal(further), None, part).start()
            copy(slot, across, None, part).start()
    slot = rcv_slot(0, True)
    for part in range(PARTS):
        arrive(slot, part)
        for device in (along(1), along(-1)):
            copy(slot, device, None, part).start()
    for index in range(8):
        arrive((1 - core) * 8 + index)
    local.wait()
    half = src_ref.shape[1]
    quarter = half // 2
    flags_ref[0:half, :] = unpack(
        half, lambda p: p, lambda p: 4 * channel_group(p), pieces, ordered, left)
    for block in range(blocks):
        transform(block, left, table, spectrum, high, low_part)
    for block in range(blocks):
        put_sources(block, spectrum, high, low_part, seed, src_ref)
    loads[4].wait()
    views = [ref.at[0:half] for ref in (spectrum, high, low_part)]
    for batch, column in enumerate((own_low, 1 - own_low)):
        for step in range(8):
            if step not in ((0, 2, 6), (0,))[batch]:
                arrive(rcv_slot(step, batch == 1), 0)
        base = 16 + 8 * column
        first = quarter * column
        flags_ref[pl.ds(pl.multiple_of(half + first, quarter), quarter), :] = unpack(
            quarter, lambda p: base + p, lambda p: 4 * p, pieces, ordered, left)
        if batch == 1:
            flip = flags_ref[0:half, :].T
            counts = sum(flags_ref[half : 2 * half, w : w + 1] * flip[w : w + 1, :] for w in range(WIN))
            scale = mask[...].astype(F32).T * (1.0 / math.sqrt(NF)) / jnp.maximum(counts, 1.0)
            weights_ref[...] = jnp.concatenate([scale, jnp.zeros((half, 128 - half), F32)], axis=1)
        for block in range(blocks):
            transform(block, left, table, *views)
        for block in range(blocks):
            put_receivers(block, *views, first, rcv_ref)
    block = pieces.at[pl.ds(0, 30)]
    pltpu.make_async_copy(block, block, send_sems.at[0]).wait()

    @pl.when(away)
    def _():
        for part in range(PARTS):
            mirrored[part].wait_send()


def spectra(half, traces, window_valid, pair_mask):
    seed, lag_seed = seeds()
    total = WIN * half
    far = pl.BlockSpec(memory_space=pltpu.HBM)
    rows = 2 * WIN * traces.shape[1]
    return pl.pallas_call(
        spectra_kernel,
        out_shape=[
            jax.ShapeDtypeStruct((WIN, half, 3 * NF), F32),
            jax.ShapeDtypeStruct((WIN, half, 3 * NF), BF16),
            jax.ShapeDtypeStruct((half, 128), F32),
            jax.ShapeDtypeStruct((NF, LAGS // 2), BF16),
            jax.ShapeDtypeStruct((NF, LAGS // 2), BF16),
        ],
        in_specs=[far] * 5,
        out_specs=[VMEM] * 5,
        scratch_shapes=[
            pltpu.VMEM(traces.shape, BF16),
            pltpu.VMEM(window_valid.shape, jnp.int32),
            pltpu.VMEM(seed.shape, F32),
            pltpu.VMEM(lag_seed.shape, F32),
            pltpu.VMEM(pair_mask.shape, jnp.int32),
            pltpu.VMEM((2 * half, 128), F32),
            pltpu.VMEM((PARTS, rows, NS // 2 // PARTS), BF16),
            pltpu.VMEM((32, PARTS, rows, NS // 2 // PARTS), BF16),
            pltpu.VMEM((NS // 2, NS), BF16),
            pltpu.VMEM((4, half, NS // 2), F32),
            pltpu.VMEM((2 * total, NS // 2), BF16),
            pltpu.VMEM((total, NS), F32),
            pltpu.VMEM((total, NF + 256), BF16),
            pltpu.VMEM((total, NF + 256), BF16),
            pltpu.SemaphoreType.DMA((5,)),
            pltpu.SemaphoreType.DMA((1 + PARTS,)),
            pltpu.SemaphoreType.DMA((32, PARTS)),
        ],
        compiler_params=pltpu.CompilerParams(
            collective_id=0, has_side_effects=True, vmem_limit_bytes=28 * 2**20),
    )(*(pltpu.with_memory_space_constraint(a, pltpu.HBM) for a in (traces, window_valid, jnp.asarray(seed), jnp.asarray(lag_seed), pair_mask)))


def shards(traces, window_valid, pair_mask):
    src, rcv, weights, cos_table, sin_table = spectra(pair_mask.shape[0], traces, window_valid, pair_mask)
    return correlated(src, rcv, weights, cos_table, sin_table)


def solution(mesh):
    in_specs = (P(None, ("src", "rcv"), None), P(None, ("src", "rcv")), P("src", "rcv"))
    mapped = jax.shard_map(
        shards, mesh=mesh, in_specs=in_specs, out_specs=P("src", "rcv", None), check_vma=False)

    def run(traces, window_valid, pair_mask):
        with jax.sharding.use_abstract_mesh(mesh.abstract_mesh):
            return mapped(traces, window_valid, pair_mask)

    return run
```
